128 devices in a mesh: lat: 8 (over x_hi, y), lon: 16 (over z, x_lo, core).
Axes of the slice: x: 4 (x_hi: 2, x_lo: 2; x = x_hi * 2 + x_lo), y: 4, z: 4, core: 2. Of those that a mesh axis runs over, the one named last changes fastest.
Arguments:
- tokens: float32 [4, 192, 384, 512], P(None, 'lat', 'lon'), may hold values from -6 to 6
- region: int32 [4, 192, 384], P(None, 'lat', 'lon'), may hold values from 0 to 2
- rel_index: int32 [144, 144], replicated, may hold values from 0 to 758
- rel_table: float32 [8, 759], replicated, may hold values from -5 to 5
- norm1_gain: float32 [512], replicated, may hold values from 0.1 to 1.9
- norm1_bias: float32 [512], replicated, may hold values from -3 to 3
- qkv_weight: bfloat16 [512, 1536], replicated, may hold values from -2.2 to 2.2
- qkv_bias: float32 [1536], replicated, may hold values from -3 to 3
- proj_weight: bfloat16 [512, 512], replicated, may hold values from -0.25 to 0.25
- proj_bias: float32 [512], replicated, may hold values from -3 to 3
- norm2_gain: float32 [512], replicated, may hold values from 0.1 to 1.9
- norm2_bias: float32 [512], replicated, may hold values from -3 to 3
- fc1_weight: bfloat16 [512, 2048], replicated, may hold values from -0.25 to 0.25
- fc1_bias: float32 [2048], replicated, may hold values from -3 to 3
- fc2_weight: bfloat16 [2048, 512], replicated, may hold values from -0.125 to 0.125
- fc2_bias: float32 [512], replicated, may hold values from -3 to 3
- merge_gain: float32 [2048], replicated, may hold values from 0.1 to 1.9
- merge_bias: float32 [2048], replicated, may hold values from -3 to 3
- merge_weight: bfloat16 [2048, 1024], replicated, may hold values from -0.125 to 0.125
Outputs:
- merged: bfloat16 [4, 96, 192, 1024], P(None, 'lat', 'lon')
The draws below stay inside these ranges and needn't reach their ends.
All inputs are finite; a program needn't handle non-finite values.
Results may differ from the reference program's by a relative error of at most 0.012.
The reference program's roundings to bfloat16 on the way (of `normed1`, `packed`, `weights`, `attended`, `normed2`, `activated` and `normed3`) count: a program that leaves them out, or rounds other values in their place, can miss the bound.
Values sent between devices are 32-bit elements; how exact they have to be, the bound alone decides.
A program may use at most 192 MiB of HBM per device.

```python
import jax
import jax.numpy as jnp
from jax import lax

D = 512
HEADS = 8
FFN = 2048
MERGED = 1024
LEV = 4
WL = 2
WH = 6
WW = 12
WTOK = 144
RELN = 759
NLAT = 192
NLON = 384


def draw_qkv_weight(key, part):
    key = jax.random.fold_in(key, 7)
    base = jax.random.truncated_normal(key, -4.0, 4.0, (D, 3 * D), jnp.float32) * D ** (-0.5)
    return base.astype(jnp.bfloat16)


def touch_ends(array, rng, smallest, largest):
    extent = array.shape
    index_at = [jax.random.randint(jax.random.fold_in(rng, axis), (), 0, extent[axis]) for axis in range(len(extent))]
    array = array.at[tuple(index_at)].set(smallest)
    longest = extent.index(max(extent))
    index_at[longest] = (index_at[longest] + 1) % extent[longest]
    return array.at[tuple(index_at)].set(largest)


def steps_of(key, dims, cuts, low, top_value):
    gain, own = 1.0, jax.random.fold_in(key, 6)
    for axis_at, shards_of in cuts:
        steps = jnp.exp(jax.random.uniform(jax.random.fold_in(own, axis_at), (shards_of,), jnp.float32, low / len(cuts), top_value / len(cuts)))
        gain = gain * jnp.repeat(steps, dims[axis_at] // shards_of).reshape([-1 if axis == axis_at else 1 for axis in range(len(dims))])
    return gain


def bell_draw(rng, shape, scale, most, shards=(), held_as=jnp.bfloat16):
    array = scale * jax.random.normal(rng, shape, jnp.float32)
    if shards:
        array = array * steps_of(rng, shape, shards, -0.22, 0.18)
    return jnp.clip(array, -most, most).astype(held_as)


def setup_inputs(seed: int = 0) -> dict:
    arg_keys = jax.random.split(jax.random.key(seed), 20)
    return {
        "tokens": bell_draw(arg_keys[0], (LEV, NLAT, NLON, D), 1.0, 6.0, ((1, 8), (2, 16)), jnp.float32),
        "region": touch_ends(jax.random.randint(arg_keys[1], (LEV, NLAT, NLON), 0, 3), jax.random.fold_in(arg_keys[1], 1), 0, 2).astype(jnp.int32),
        "rel_index": touch_ends(jax.random.randint(arg_keys[2], (WTOK, WTOK), 0, RELN), jax.random.fold_in(arg_keys[2], 1), 0, RELN - 1).astype(jnp.int32),
        "rel_table": bell_draw(arg_keys[3], (HEADS, RELN), 1.0, 5.0, (), jnp.float32),
        "norm1_gain": jnp.clip(1.0 + 0.18 * jax.random.normal(arg_keys[4], (D,), jnp.float32), 0.1, 1.9),
        "norm1_bias": bell_draw(arg_keys[5], (D,), 0.5, 3.0, (), jnp.float32),
        "qkv_weight": draw_qkv_weight(jax.random.fold_in(arg_keys[19], 71), 0),
        "qkv_bias": bell_draw(arg_keys[7], (3 * D,), 0.5, 3.0, (), jnp.float32),
        "proj_weight": bell_draw(arg_keys[8], (D, D), D ** -0.5, 0.25),
        "proj_bias": bell_draw(arg_keys[9], (D,), 0.5, 3.0, (), jnp.float32),
        "norm2_gain": jnp.clip(1.0 + 0.18 * jax.random.normal(arg_keys[10], (D,), jnp.float32), 0.1, 1.9),
        "norm2_bias": bell_draw(arg_keys[11], (D,), 0.5, 3.0, (), jnp.float32),
        "fc1_weight": bell_draw(arg_keys[12], (D, FFN), D ** -0.5, 0.25),
        "fc1_bias": bell_draw(arg_keys[13], (FFN,), 0.5, 3.0, (), jnp.float32),
        "fc2_weight": bell_draw(arg_keys[14], (FFN, D), FFN ** -0.5, 0.125),
        "fc2_bias": bell_draw(arg_keys[15], (D,), 0.5, 3.0, (), jnp.float32),
        "merge_gain": jnp.clip(1.0 + 0.18 * jax.random.normal(arg_keys[16], (4 * D,), jnp.float32), 0.1, 1.9),
        "merge_bias": bell_draw(arg_keys[17], (4 * D,), 0.5, 3.0, (), jnp.float32),
        "merge_weight": bell_draw(arg_keys[18], (4 * D, MERGED), (4 * D) ** -0.5, 0.125),
    }


EPS = 1e-05

def layer_norm(values, norm_gain, norm_bias):
    centre_val = lax.optimization_barrier(jnp.mean(values, -1, keepdims=True))
    centred = values - centre_val
    variance = lax.optimization_barrier(jnp.mean(centred * centred, -1, keepdims=True))
    return centred * lax.rsqrt(variance + EPS) * norm_gain + norm_bias

def windows_of(field):
    lev_count, row_count, col_count = field.shape[:3]
    trailing = field.shape[3:]
    blocks = field.reshape((lev_count // WL, WL, row_count // WH, WH, col_count // WW, WW) + trailing)
    order_axes = (2, 4, 0, 1, 3, 5) + tuple(range(6, 6 + len(trailing)))
    return blocks.transpose(order_axes).reshape((-1, WL * WH * WW) + trailing)

def frame_of(wins, lev_count, row_count, col_count):
    trailing = wins.shape[2:]
    blocks = wins.reshape((row_count // WH, col_count // WW, lev_count // WL, WL, WH, WW) + trailing)
    order_axes = (2, 3, 0, 4, 1, 5) + tuple(range(6, 6 + len(trailing)))
    return blocks.transpose(order_axes).reshape((lev_count, row_count, col_count) + trailing)

def window_block(wins, region_ids, band_ids, usable, params):
    rel_index, rel_table, norm1_gain, norm1_bias, qkv_weight, qkv_bias, proj_weight, proj_bias, norm2_gain, norm2_bias, fc1_weight, fc1_bias, fc2_weight, fc2_bias = params
    win_count, win_tokens, width = wins.shape
    num_heads = rel_table.shape[0]
    head_size = width // num_heads
    tokens_flat = wins.reshape(win_count * win_tokens, width)
    normed1 = layer_norm(tokens_flat, norm1_gain, norm1_bias).astype(jnp.bfloat16)
    packed = (jnp.dot(normed1, qkv_weight, preferred_element_type=jnp.float32) + qkv_bias).astype(jnp.bfloat16)
    packed = packed.reshape(win_count, win_tokens, 3, num_heads, head_size)
    queries = packed[:, :, 0].astype(jnp.float32)
    key_heads = packed[:, :, 1].astype(jnp.float32)
    values = packed[:, :, 2].astype(jnp.float32)
    scores = jnp.einsum('nahd,nbhd->nhab', queries, key_heads) * head_size ** (-0.5)
    scores = scores + rel_table[:, rel_index][None]
    allowed = (region_ids[:, :, None] == region_ids[:, None, :]) & (band_ids[:, :, None] == band_ids[:, None, :]) & usable[:, None, :]
    scores = jnp.where(allowed[:, None], scores, jnp.float32(-1e+30))
    row_max = lax.optimization_barrier(jnp.max(scores, -1, keepdims=True))
    powers = jnp.exp(scores - row_max)
    weights = (powers / lax.optimization_barrier(jnp.sum(powers, -1, keepdims=True))).astype(jnp.bfloat16)
    attended = jnp.einsum('nhab,nbhd->nahd', weights.astype(jnp.float32), values).astype(jnp.bfloat16)
    attended = attended.reshape(win_count * win_tokens, width)
    hidden = jnp.dot(attended, proj_weight, preferred_element_type=jnp.float32) + proj_bias + tokens_flat
    normed2 = layer_norm(hidden, norm2_gain, norm2_bias).astype(jnp.bfloat16)
    activated = jax.nn.gelu(jnp.dot(normed2, fc1_weight, preferred_element_type=jnp.float32) + fc1_bias, approximate=False).astype(jnp.bfloat16)
    result = jnp.dot(activated, fc2_weight, preferred_element_type=jnp.float32) + fc2_bias + hidden
    return result.reshape(win_count, win_tokens, width)

def merge_patches(field, merge_gain, merge_bias, merge_weight):
    lev_count, row_count, col_count, width = field.shape
    grouped = field.reshape(lev_count, row_count // 2, 2, col_count // 2, 2, width)
    grouped = grouped.transpose(0, 1, 3, 4, 2, 5).reshape(lev_count, row_count // 2, col_count // 2, 4 * width)
    normed3 = layer_norm(grouped, merge_gain, merge_bias).astype(jnp.bfloat16)
    product = jnp.dot(normed3.reshape(-1, 4 * width), merge_weight, preferred_element_type=jnp.float32)
    return product.astype(jnp.bfloat16).reshape(lev_count, row_count // 2, col_count // 2, -1)

def reference(tokens, region, rel_index, rel_table, norm1_gain, norm1_bias, qkv_weight, qkv_bias, proj_weight, proj_bias, norm2_gain, norm2_bias, fc1_weight, fc1_bias, fc2_weight, fc2_bias, merge_gain, merge_bias, merge_weight):
    params = (rel_index, rel_table, norm1_gain, norm1_bias, qkv_weight, qkv_bias, proj_weight, proj_bias, norm2_gain, norm2_bias, fc1_weight, fc1_bias, fc2_weight, fc2_bias)
    half_rows = WH // 2
    half_cols = WW // 2
    shifted = jnp.roll(jnp.roll(jnp.roll(tokens, -1, 0), half_rows, 1), half_cols, 2)
    region_ids = jnp.roll(jnp.roll(jnp.roll(region, -1, 0), half_rows, 1), half_cols, 2)
    wrapped = jnp.mod(jnp.arange(NLAT, dtype=jnp.int32) - half_rows, NLAT)
    lat_band = (wrapped >= NLAT - half_rows).astype(jnp.int32)
    lev_band = (jnp.arange(LEV, dtype=jnp.int32) == LEV - 1).astype(jnp.int32)
    band_ids = jnp.broadcast_to(lev_band[:, None, None] * 2 + lat_band[None, :, None], (LEV, NLAT, NLON))
    stacked = shifted.reshape(LEV, NLAT // WH, WH, NLON, D).transpose(1, 0, 2, 3, 4)
    stacked_ids = region_ids.reshape(LEV, NLAT // WH, WH, NLON).transpose(1, 0, 2, 3)
    stacked_bands = band_ids.reshape(LEV, NLAT // WH, WH, NLON).transpose(1, 0, 2, 3)

    def one_band(pieces):
        piece_tokens, piece_ids, piece_bands = pieces
        win_ids = windows_of(piece_ids)
        usable = jnp.ones(win_ids.shape, dtype=bool)
        result = window_block(windows_of(piece_tokens), win_ids, windows_of(piece_bands), usable, params)
        return frame_of(result, LEV, WH, NLON)
    finished = lax.map(one_band, (stacked, stacked_ids, stacked_bands))
    block_out = finished.transpose(1, 0, 2, 3, 4).reshape(LEV, NLAT, NLON, D)
    restored = jnp.roll(jnp.roll(jnp.roll(block_out, 1, 0), -half_rows, 1), -half_cols, 2)
    return merge_patches(restored, merge_gain, merge_bias, merge_weight)
```

```python
import functools

import jax
import jax.numpy as jnp
from jax import lax
from jax.experimental import pallas as pl
from jax.experimental.pallas import tpu as pltpu
from jax.sharding import PartitionSpec as P

MESH = pl.DeviceIdType.MESH
F32 = jnp.float32
BF16 = jnp.bfloat16
EPS = 1e-05
SIDE = 24
WTOK = 144
G = 4
ROWS = G * WTOK
TOKENS = 4 * SIDE * SIDE
TILES = 4
SLOT = 72

LEVELS = ((1, 2), (3, 0))
CORNER = ((-3, -6), (3, 6))
PIECES = (
    ((3, 6, 18, 6), (9, 6, 18, 6), (15, 6, 18, 6), (0, 3, 18, 6), (21, 3, 6, 12), (21, 3, 0, 6), (21, 3, 18, 6)),
    ((3, 6, 0, 6), (9, 6, 0, 6), (15, 6, 0, 6), (21, 3, 0, 6), (0, 3, 6, 12), (0, 3, 18, 6), (0, 3, 0, 6)),
)
FROM = ((0, -1), (0, -1), (0, -1), (0, -1), (-1, 0), (-1, 0), (-1, -1))
STEPS = (
    ((0, 1, 1), (0, 2, 1), (1, 0, 0), (1, 1, 0)),
    ((0, 1, 0), (0, 2, 0), (1, 0, 1), (1, 1, 1)),
    ((0, 0, 0), (0, 0, 1), (1, 3, 1), (1, 3, 0)),
    ((0, 3, 0), (1, 2, 1), (0, 3, 1), (1, 2, 0)),
)


def segments(window):
    pair, wrow, wcol = window
    row0, col0 = CORNER[pair][0] + 6 * wrow, CORNER[pair][1] + 12 * wcol
    runs = []
    for lev in range(2):
        for row in range(6):
            for half in range(2):
                at_row, at_col = row0 + row, col0 + 6 * half
                where_row, where_col = at_row % SIDE, at_col % SIDE
                away = (at_row // SIDE, at_col // SIDE)
                token = (lev * 6 + row) * 12 + 6 * half
                if away == (0, 0):
                    slot, first = None, (LEVELS[pair][lev] * SIDE + where_row) * SIDE + where_col
                else:
                    slot = None
                    for number, (first_row, rows, first_col, cols) in enumerate(PIECES[pair]):
                        if first_row <= where_row < first_row + rows and first_col <= where_col < first_col + cols:
                            slot = number
                            first = (lev * rows + where_row - first_row) * cols + where_col - first_col
                if runs and runs[-1][2] == slot and runs[-1][0] + runs[-1][1] == token and runs[-1][3] + runs[-1][1] == first:
                    runs[-1] = (runs[-1][0], runs[-1][1] + 6, slot, runs[-1][3])
                else:
                    runs.append((token, 6, slot, first))
    return runs


def slots_of(windows):
    return [
        (window[0], slot)
        for window in windows
        for slot in sorted({run[2] for run in segments(window) if run[2] is not None})
    ]


def piece_runs(pair, slot):
    first_row, rows, first_col, cols = PIECES[pair][slot]
    for lev in range(2):
        for row in range(rows):
            yield (lev * rows + row) * cols, cols, (LEVELS[pair][lev] * SIDE + first_row + row) * SIDE + first_col


def norm(values, gain, shift):
    centred = values - jnp.mean(values, -1, keepdims=True)
    variance = jnp.mean(centred * centred, -1, keepdims=True)
    return centred * lax.rsqrt(variance + EPS) * gain + shift


def wide(ref, first, count):
    return jnp.concatenate([ref[tile, pl.ds(first, count), :] for tile in range(TILES)], 1)


def put_wide(ref, first, count, values):
    for tile in range(TILES):
        ref[tile, pl.ds(first, count), :] = values[:, 128 * tile : 128 * (tile + 1)]


def make_bias(rel_index, rel_table, bias):
    def rows_at(step, _):
        at = pl.multiple_of(step * 8, 8)
        for first, count in ((0, 128), (128, 16)):
            index = rel_index[pl.ds(at, 8), pl.ds(first, count)]
            if count < 128:
                index = jnp.concatenate([index, jnp.zeros((8, 128 - count), jnp.int32)], 1)
            low, high = index & 127, index >> 7
            for head in range(8):
                found = jnp.zeros((8, 128), F32)
                for part in range(6):
                    row = rel_table[pl.ds(head, 1), pl.ds(128 * part, 128)]
                    drawn = jnp.take_along_axis(
                        jnp.broadcast_to(row, (8, 128)), low, axis=1, mode="promise_in_bounds"
                    )
                    found = jnp.where(high == part, drawn, found)
                bias[head, pl.ds(at, 8), pl.ds(first, count)] = found[:, :count]
        return 0

    lax.fori_loop(0, WTOK // 8, rows_at, 0)


def attend(qkv, attended, bias, marks, first):
    lane = lax.broadcasted_iota(jnp.int32, (1, 128), 1)
    left = lane < 64
    mark = marks[pl.ds(first, WTOK), :]
    barred = jnp.where(mark > 0, jnp.zeros_like(mark), jnp.full_like(mark, -1e30))
    ones = jnp.ones((WTOK, 128), BF16)
    for pair in range(4):
        query = qkv[pl.ds(first, WTOK), pl.ds(128 * pair, 128)]
        key = qkv[pl.ds(first, WTOK), pl.ds(512 + 128 * pair, 128)]
        value = qkv[pl.ds(first, WTOK), pl.ds(1024 + 128 * pair, 128)]
        keys = jnp.concatenate([key, barred], 1)
        values = jnp.concatenate([value, ones], 1)
        zero = jnp.zeros_like(query)
        results = []
        for side in range(2):
            part = jnp.where(left, query, zero) if side == 0 else jnp.where(left, zero, query)
            scores = lax.dot_general(
                jnp.concatenate([part, mark], 1), keys, (((1,), (1,)), ((), ())), preferred_element_type=F32
            )
            scores = scores + bias[2 * pair + side]
            powers = jnp.exp(scores - jnp.max(scores, -1, keepdims=True)).astype(BF16)
            total = jnp.dot(powers, values, preferred_element_type=F32)
            results.append(total[:, :128] / total[:, 128:])
        attended[pl.ds(first, WTOK), pl.ds(128 * pair, 128)] = jnp.where(left, results[0], results[1]).astype(BF16)


def mark_window(ids, marks, window, first, lat, lat_count):
    pair, wrow, wcol = window
    row0, col0 = CORNER[pair][0] + 6 * wrow, CORNER[pair][1] + 12 * wcol
    token = lax.broadcasted_iota(jnp.int32, (WTOK, 1), 0)
    lev, row, col = token // 72, token // 12 % 6, token % 12
    at_row = row0 + row
    line = lev * SIDE + (at_row + SIDE) % SIDE
    pick = lax.broadcasted_iota(jnp.int32, (WTOK, 2 * SIDE), 1) == line
    rows = jnp.dot(jnp.where(pick, 1.0, 0.0).astype(BF16), ids[pair].astype(BF16), preferred_element_type=F32)
    lane = lax.broadcasted_iota(jnp.int32, (WTOK, 128), 1)
    region = jnp.sum(jnp.where(lane == (col0 + col + SIDE) % SIDE, rows, 0.0), -1, keepdims=True)
    whole = lat_count * SIDE
    orig = lat * SIDE + at_row
    orig = jnp.where(orig < 0, orig + whole, jnp.where(orig >= whole, orig - whole, orig))
    band = jnp.where(orig >= whole - 3, 1, 0)
    if pair == 1:
        band = band + 2 * lev
    kind = region.astype(jnp.int32) + 3 * band
    marks[pl.ds(first, WTOK), :] = jnp.where(lane == kind, 1.0, 0.0).astype(BF16)


def kernel(
    lat_count,
    lon_count,
    tokens,
    qkv_weight,
    proj_weight,
    fc1_weight,
    fc2_weight,
    merge_weight,
    region,
    rel_index,
    rel_table,
    norm1_gain,
    norm1_bias,
    qkv_bias,
    proj_bias,
    norm2_gain,
    norm2_bias,
    fc1_bias,
    fc2_bias,
    merge_gain,
    merge_bias,
    out,
    block,
    part,
    wq,
    wp,
    w1,
    w2,
    wm,
    bias,
    marks,
    normed,
    qkv,
    attended,
    active,
    normed3,
    own_ids,
    far_ids,
    ids,
    halo_out,
    halo_in,
    back_out,
    back_in,
    load_sem,
    id_send,
    id_recv,
    halo_send,
    halo_recv,
    back_send,
    back_recv,
):
    lat, lon = lax.axis_index("lat"), lax.axis_index("lon")

    def device(rows, cols):
        return lax.rem(lat + rows + lat_count, lat_count), lax.rem(lon + cols + lon_count, lon_count)

    barrier = pltpu.get_barrier_semaphore()
    around = ((0, 1), (1, 0), (1, 1), (0, -1), (-1, 0), (-1, -1))
    for away in around:
        pl.semaphore_signal(barrier, inc=1, device_id=device(*away), device_id_type=MESH)

    loads = [
        pltpu.make_async_copy(
            tokens.at[:, pl.ds(128 * tile, 128)], block.at[tile, pl.ds(0, TOKENS)], load_sem.at[tile]
        )
        for tile in range(TILES)
    ]
    for number, (source, target) in enumerate(
        ((qkv_weight, wq), (proj_weight, wp), (fc1_weight, w1), (fc2_weight, w2), (merge_weight, wm))
    ):
        loads.append(pltpu.make_async_copy(source, target, load_sem.at[TILES + number]))
    for load in loads:
        load.start()

    own_ids[...] = jnp.zeros_like(own_ids)
    for pair in range(2):
        for lev in range(2):
            own_ids[pair, pl.ds(SIDE * lev, SIDE), pl.ds(0, SIDE)] = region[LEVELS[pair][lev]].astype(F32)
    block[:, pl.ds(TOKENS, 16), :] = jnp.zeros((TILES, 16, 128), F32)
    for pair in range(2):
        for slot in (3, 5, 6):
            halo_out[pair, slot, :, pl.ds(32, 8), :] = jnp.zeros((TILES, 8, 128), F32)
            back_out[pair, slot, :, pl.ds(32, 8), :] = jnp.zeros((TILES, 8, 128), F32)

    def id_copy(pair, side):
        rows, cols = ((0, 1), (1, 0), (1, 1))[side]
        sign = 1 if pair == 0 else -1
        return pltpu.make_async_remote_copy(
            src_ref=own_ids.at[pair],
            dst_ref=far_ids.at[pair, side],
            send_sem=id_send.at[pair, side],
            recv_sem=id_recv.at[pair, side],
            device_id=device(sign * rows, sign * cols),
            device_id_type=MESH,
        )

    def piece_copy(pair, slot, back):
        rows, cols = FROM[slot]
        sign = (1 if pair == 0 else -1) * (1 if back else -1)
        size = SLOT if slot in (0, 1, 2, 4) else 40
        source, target = (back_out, back_in) if back else (halo_out, halo_in)
        send, recv = (back_send, back_recv) if back else (halo_send, halo_recv)
        return pltpu.make_async_remote_copy(
            src_ref=source.at[pair, slot, :, pl.ds(0, size)],
            dst_ref=target.at[pair, slot, :, pl.ds(0, size)],
            send_sem=send.at[pair, slot],
            recv_sem=recv.at[pair, slot],
            device_id=device(sign * rows, sign * cols),
            device_id_type=MESH,
        )

    order = [slot for step in STEPS for slot in slots_of(step)]

    pl.semaphore_wait(barrier, len(around))
    for pair in range(2):
        for side in range(3):
            id_copy(pair, side).start()
    for load in loads[:TILES]:
        load.wait()
    for pair, slot in order:
        for first, count, where in piece_runs(pair, slot):
            halo_out[pair, slot, :, pl.ds(first, count), :] = block[:, pl.ds(where, count), :]
        piece_copy(pair, slot, False).start()

    make_bias(rel_index, rel_table, bias)

    for pair in range(2):
        for side in range(3):
            id_copy(pair, side).wait()
        line = lax.broadcasted_iota(jnp.int32, (2 * SIDE, 128), 0) % SIDE
        lane = lax.broadcasted_iota(jnp.int32, (2 * SIDE, 128), 1)
        far_row = line >= SIDE - 3 if pair == 0 else line < 3
        far_col = lane >= SIDE - 6 if pair == 0 else lane < 6
        ids[pair] = jnp.where(
            far_row,
            jnp.where(far_col, far_ids[pair, 2], far_ids[pair, 1]),
            jnp.where(far_col, far_ids[pair, 0], own_ids[pair]),
        )
    for load in loads[TILES:-1]:
        load.wait()

    def run(step, _):
        for number, windows in enumerate(STEPS):

            @pl.when(step == number)
            def _():
                for pair, slot in slots_of(windows):
                    piece_copy(pair, slot, False).wait_recv()
                for place, window in enumerate(windows):
                    for token, count, slot, first in segments(window):
                        at = pl.ds(place * WTOK + token, count)
                        if slot is None:
                            part[:, at, :] = block[:, pl.ds(first, count), :]
                        else:
                            part[:, at, :] = halo_in[window[0], slot, :, pl.ds(first, count), :]
                    mark_window(ids, marks, window, place * WTOK, lat, lat_count)

        for place in range(G):
            normed[pl.ds(place * WTOK, WTOK), :] = norm(
                wide(part, place * WTOK, WTOK), norm1_gain[...], norm1_bias[...]
            ).astype(BF16)
        for third in range(3):
            columns = pl.ds(512 * third, 512)
            packed = jnp.dot(normed[...], wq[:, columns], preferred_element_type=F32) + qkv_bias[:, columns]
            if third == 0:
                packed = packed * 0.125
            qkv[:, columns] = packed.astype(BF16)
        for place in range(G):
            attend(qkv, attended, bias, marks, place * WTOK)
        hidden = jnp.dot(attended[...], wp[...], preferred_element_type=F32) + proj_bias[...] + wide(part, 0, ROWS)
        put_wide(part, 0, ROWS, hidden)
        normed[...] = norm(hidden, norm2_gain[...], norm2_bias[...]).astype(BF16)
        for quarter in range(4):
            columns = pl.ds(512 * quarter, 512)
            units = jnp.dot(normed[...], w1[:, columns], preferred_element_type=F32) + fc1_bias[:, columns]
            active[:, columns] = (0.5 * units * (1.0 + lax.erf(units * 0.7071067811865476))).astype(BF16)
        result = jnp.dot(active[...], w2[...], preferred_element_type=F32) + fc2_bias[...] + wide(part, 0, ROWS)
        put_wide(part, 0, ROWS, result)

        for number, windows in enumerate(STEPS):

            @pl.when(step == number)
            def _():
                for place, window in enumerate(windows):
                    for token, count, slot, first in segments(window):
                        at = pl.ds(place * WTOK + token, count)
                        if slot is None:
                            block[:, pl.ds(first, count), :] = part[:, at, :]
                        else:
                            back_out[window[0], slot, :, pl.ds(first, count), :] = part[:, at, :]
                for pair, slot in slots_of(windows):
                    piece_copy(pair, slot, True).start()

        return 0

    lax.fori_loop(0, len(STEPS), run, 0)

    for pair, slot in order:
        piece_copy(pair, slot, True).wait_recv()
        for first, count, where in piece_runs(pair, slot):
            block[:, pl.ds(where, count), :] = back_in[pair, slot, :, pl.ds(first, count), :]
    loads[-1].wait()

    def merge_norm(step, _):
        for number in range(4):
            line = step * 4 + number
            values = jnp.concatenate(
                [
                    block[tile, pl.ds(line * 2 * SIDE + row * SIDE + col, 16, stride=2), :]
                    for col in range(2)
                    for row in range(2)
                    for tile in range(TILES)
                ],
                1,
            )
            normed3[pl.ds(pl.multiple_of(line * 16, 16), 16), :] = norm(
                values, merge_gain[...], merge_bias[...]
            ).astype(BF16)
        return 0

    lax.fori_loop(0, 12, merge_norm, 0)
    for quarter in range(4):
        columns = pl.ds(256 * quarter, 256)
        merged = jnp.dot(normed3[...], wm[:, columns], preferred_element_type=F32).astype(BF16)
        out[:, :, columns] = merged.reshape(48, 16, 256)[:, :12]

    for pair, slot in order:
        piece_copy(pair, slot, False).wait_send()
        piece_copy(pair, slot, True).wait_send()


def per_device(mesh_shape, tokens, region, rel_index, rel_table, *rest):
    (
        norm1_gain,
        norm1_bias,
        qkv_weight,
        qkv_bias,
        proj_weight,
        proj_bias,
        norm2_gain,
        norm2_bias,
        fc1_weight,
        fc1_bias,
        fc2_weight,
        fc2_bias,
        merge_gain,
        merge_bias,
        merge_weight,
    ) = rest
    lines = [
        value.reshape(1, -1)
        for value in (
            norm1_gain,
            norm1_bias,
            qkv_bias,
            proj_bias,
            norm2_gain,
            norm2_bias,
            fc1_bias,
            fc2_bias,
            merge_gain,
            merge_bias,
        )
    ]
    rel_table = jnp.pad(rel_table, ((0, 0), (0, 768 - rel_table.shape[1])))
    hbm = pl.BlockSpec(memory_space=pl.ANY)
    vmem = pl.BlockSpec(memory_space=pltpu.VMEM)
    merged = pl.pallas_call(
        functools.partial(kernel, *mesh_shape),
        out_shape=jax.ShapeDtypeStruct((48, 12, 1024), BF16),
        in_specs=[hbm] * 6 + [vmem] * 13,
        out_specs=vmem,
        scratch_shapes=[
            pltpu.VMEM((TILES, TOKENS + 16, 128), F32),
            pltpu.VMEM((TILES, ROWS, 128), F32),
            pltpu.VMEM((512, 1536), BF16),
            pltpu.VMEM((512, 512), BF16),
            pltpu.VMEM((512, 2048), BF16),
            pltpu.VMEM((2048, 512), BF16),
            pltpu.VMEM((2048, 1024), BF16),
            pltpu.VMEM((8, WTOK, WTOK), F32),
            pltpu.VMEM((ROWS, 128), BF16),
            pltpu.VMEM((ROWS, 512), BF16),
            pltpu.VMEM((ROWS, 1536), BF16),
            pltpu.VMEM((ROWS, 512), BF16),
            pltpu.VMEM((ROWS, 2048), BF16),
            pltpu.VMEM((768, 2048), BF16),
            pltpu.VMEM((2, 2 * SIDE, 128), F32),
            pltpu.VMEM((2, 3, 2 * SIDE, 128), F32),
            pltpu.VMEM((2, 2 * SIDE, 128), F32),
        ]
        + [pltpu.VMEM((2, 7, TILES, SLOT, 128), F32)] * 4
        + [
            pltpu.SemaphoreType.DMA((TILES + 5,)),
            pltpu.SemaphoreType.DMA((2, 3)),
            pltpu.SemaphoreType.DMA((2, 3)),
        ]
        + [pltpu.SemaphoreType.DMA((2, 7))] * 4,
        compiler_params=pltpu.CompilerParams(
            collective_id=0, has_side_effects=True, vmem_limit_bytes=60 * 2**20
        ),
        name="block",
    )(
        tokens.reshape(TOKENS, 512),
        qkv_weight,
        proj_weight,
        fc1_weight,
        fc2_weight,
        merge_weight,
        region,
        rel_index,
        rel_table,
        *lines,
    )
    return merged.reshape(4, 12, 12, 1024)


def solution(mesh):
    shape = (mesh.shape["lat"], mesh.shape["lon"])
    return jax.shard_map(
        functools.partial(per_device, shape),
        mesh=mesh,
        in_specs=(P(None, "lat", "lon", None), P(None, "lat", "lon")) + (P(),) * 17,
        out_specs=P(None, "lat", "lon", None),
        check_vma=False,
    )
```

```python
import functools

import jax
import jax.numpy as jnp
from jax import lax
from jax.experimental import pallas as pl
from jax.experimental.pallas import tpu as pltpu
from jax.sharding import PartitionSpec as P

MESH = pl.DeviceIdType.MESH
F32 = jnp.float32
BF16 = jnp.bfloat16
EPS = 1e-05
SIDE = 24
WTOK = 144
G = 4
ROWS = G * WTOK
TOKENS = 4 * SIDE * SIDE
TILES = 4
SLOT = 72

LEVELS = ((1, 2), (3, 0))
CORNER = ((-3, -6), (3, 6))
PIECES = (
    ((3, 6, 18, 6), (9, 6, 18, 6), (15, 6, 18, 6), (0, 3, 18, 6), (21, 3, 6, 12), (21, 3, 0, 6), (21, 3, 18, 6)),
    ((3, 6, 0, 6), (9, 6, 0, 6), (15, 6, 0, 6), (21, 3, 0, 6), (0, 3, 6, 12), (0, 3, 18, 6), (0, 3, 0, 6)),
)
FROM = ((0, -1), (0, -1), (0, -1), (0, -1), (-1, 0), (-1, 0), (-1, -1))
STEPS = (
    ((0, 1, 1), (0, 2, 1), (1, 0, 0), (1, 1, 0)),
    ((0, 1, 0), (0, 2, 0), (0, 3, 0), (0, 0, 1)),
    ((0, 0, 0), (1, 3, 1), (1, 0, 1), (1, 1, 1)),
    ((1, 2, 1), (1, 3, 0), (0, 3, 1), (1, 2, 0)),
)


def segments(window):
    pair, wrow, wcol = window
    row0, col0 = CORNER[pair][0] + 6 * wrow, CORNER[pair][1] + 12 * wcol
    runs = []
    for lev in range(2):
        for row in range(6):
            for half in range(2):
                at_row, at_col = row0 + row, col0 + 6 * half
                where_row, where_col = at_row % SIDE, at_col % SIDE
                away = (at_row // SIDE, at_col // SIDE)
                token = (lev * 6 + row) * 12 + 6 * half
                if away == (0, 0):
                    slot, first = None, (LEVELS[pair][lev] * SIDE + where_row) * SIDE + where_col
                else:
                    slot = None
                    for number, (first_row, rows, first_col, cols) in enumerate(PIECES[pair]):
                        if first_row <= where_row < first_row + rows and first_col <= where_col < first_col + cols:
                            slot = number
                            first = (lev * rows + where_row - first_row) * cols + where_col - first_col
                if runs and runs[-1][2] == slot and runs[-1][0] + runs[-1][1] == token and runs[-1][3] + runs[-1][1] == first:
                    runs[-1] = (runs[-1][0], runs[-1][1] + 6, slot, runs[-1][3])
                else:
                    runs.append((token, 6, slot, first))
    return runs


def slots_of(windows):
    return [
        (window[0], slot)
        for window in windows
        for slot in sorted({run[2] for run in segments(window) if run[2] is not None})
    ]


def piece_runs(pair, slot):
    first_row, rows, first_col, cols = PIECES[pair][slot]
    for lev in range(2):
        for row in range(rows):
            yield (lev * rows + row) * cols, cols, (LEVELS[pair][lev] * SIDE + first_row + row) * SIDE + first_col


def norm(values, gain, shift):
    centred = values - jnp.mean(values, -1, keepdims=True)
    variance = jnp.mean(centred * centred, -1, keepdims=True)
    return centred * lax.rsqrt(variance + EPS) * gain + shift


def wide(ref, first, count):
    return jnp.concatenate([ref[tile, pl.ds(first, count), :] for tile in range(TILES)], 1)


def put_wide(ref, first, count, values):
    for tile in range(TILES):
        ref[tile, pl.ds(first, count), :] = values[:, 128 * tile : 128 * (tile + 1)]


def make_bias(rel_index, rel_table, table, bias):
    table[...] = jnp.zeros_like(table)
    table[:, pl.ds(0, rel_table.shape[1])] = rel_table[...]

    def rows_at(step, _):
        at = pl.multiple_of(step * 8, 8)
        for first, count in ((0, 128), (128, 16)):
            index = rel_index[pl.ds(at, 8), pl.ds(first, count)]
            if count < 128:
                index = jnp.concatenate([index, jnp.zeros((8, 128 - count), jnp.int32)], 1)
            low, high = index & 127, index >> 7
            for head in range(8):
                found = jnp.zeros((8, 128), F32)
                for part in range(6):
                    row = table[pl.ds(head, 1), pl.ds(128 * part, 128)]
                    drawn = jnp.take_along_axis(
                        jnp.broadcast_to(row, (8, 128)), low, axis=1, mode="promise_in_bounds"
                    )
                    found = jnp.where(high == part, drawn, found)
                bias[head, pl.ds(at, 8), pl.ds(first, count)] = found[:, :count]
        return 0

    lax.fori_loop(0, WTOK // 8, rows_at, 0)


def attend(qkv, attended, bias, marks, first):
    lane = lax.broadcasted_iota(jnp.int32, (1, 128), 1)
    left = lane < 64
    mark = marks[pl.ds(first, WTOK), :]
    barred = jnp.where(mark > 0, jnp.zeros_like(mark), jnp.full_like(mark, -1e30))
    ones = jnp.ones((WTOK, 128), BF16)
    for pair in range(4):
        query = qkv[pl.ds(first, WTOK), pl.ds(128 * pair, 128)]
        key = qkv[pl.ds(first, WTOK), pl.ds(512 + 128 * pair, 128)]
        value = qkv[pl.ds(first, WTOK), pl.ds(1024 + 128 * pair, 128)]
        keys = jnp.concatenate([key, barred], 1)
        values = jnp.concatenate([value, ones], 1)
        zero = jnp.zeros_like(query)
        results = []
        for side in range(2):
            part = jnp.where(left, query, zero) if side == 0 else jnp.where(left, zero, query)
            scores = lax.dot_general(
                jnp.concatenate([part, mark], 1), keys, (((1,), (1,)), ((), ())), preferred_element_type=F32
            )
            scores = scores + bias[2 * pair + side]
            powers = jnp.exp(scores - jnp.max(scores, -1, keepdims=True)).astype(BF16)
            total = jnp.dot(powers, values, preferred_element_type=F32)
            results.append(total[:, :128] / total[:, 128:])
        attended[pl.ds(first, WTOK), pl.ds(128 * pair, 128)] = jnp.where(left, results[0], results[1]).astype(BF16)


def mark_window(ids, marks, window, first, lat, lat_count):
    pair, wrow, wcol = window
    row0, col0 = CORNER[pair][0] + 6 * wrow, CORNER[pair][1] + 12 * wcol
    token = lax.broadcasted_iota(jnp.int32, (WTOK, 1), 0)
    lev, row, col = token // 72, token // 12 % 6, token % 12
    at_row = row0 + row
    line = lev * SIDE + (at_row + SIDE) % SIDE
    pick = lax.broadcasted_iota(jnp.int32, (WTOK, 2 * SIDE), 1) == line
    rows = jnp.dot(jnp.where(pick, 1.0, 0.0).astype(BF16), ids[pair].astype(BF16), preferred_element_type=F32)
    lane = lax.broadcasted_iota(jnp.int32, (WTOK, 128), 1)
    region = jnp.sum(jnp.where(lane == (col0 + col + SIDE) % SIDE, rows, 0.0), -1, keepdims=True)
    whole = lat_count * SIDE
    orig = lat * SIDE + at_row
    orig = jnp.where(orig < 0, orig + whole, jnp.where(orig >= whole, orig - whole, orig))
    band = jnp.where(orig >= whole - 3, 1, 0)
    if pair == 1:
        band = band + 2 * lev
    kind = region.astype(jnp.int32) + 3 * band
    marks[pl.ds(first, WTOK), :] = jnp.where(lane == kind, 1.0, 0.0).astype(BF16)


def kernel(
    lat_count,
    lon_count,
    tokens,
    qkv_weight,
    proj_weight,
    fc1_weight,
    fc2_weight,
    merge_weight,
    region,
    rel_index,
    rel_table,
    norm1_gain,
    norm1_bias,
    qkv_bias,
    proj_bias,
    norm2_gain,
    norm2_bias,
    fc1_bias,
    fc2_bias,
    merge_gain,
    merge_bias,
    out,
    block,
    part,
    wq,
    wp,
    w1,
    w2,
    wm,
    bias,
    marks,
    normed,
    qkv,
    attended,
    active,
    normed3,
    product,
    table,
    own_ids,
    far_ids,
    ids,
    halo_out,
    halo_in,
    back_out,
    back_in,
    load_sem,
    id_send,
    id_recv,
    halo_send,
    halo_recv,
    back_send,
    back_recv,
):
    lat, lon = lax.axis_index("lat"), lax.axis_index("lon")

    def device(rows, cols):
        return lax.rem(lat + rows + lat_count, lat_count), lax.rem(lon + cols + lon_count, lon_count)

    barrier = pltpu.get_barrier_semaphore()
    around = ((0, 1), (1, 0), (1, 1), (0, -1), (-1, 0), (-1, -1))
    for away in around:
        pl.semaphore_signal(barrier, inc=1, device_id=device(*away), device_id_type=MESH)

    def token_load(tile):
        return pltpu.make_async_copy(
            tokens.at[:, pl.ds(128 * tile, 128)], block.at[tile, pl.ds(0, TOKENS)], load_sem.at[tile]
        )

    for tile in range(TILES):
        token_load(tile).start()

    loads = [
        pltpu.make_async_copy(source, target, load_sem.at[TILES + number])
        for number, (source, target) in enumerate(
            ((qkv_weight, wq), (proj_weight, wp), (fc1_weight, w1), (fc2_weight, w2), (merge_weight, wm))
        )
    ]

    own_ids[...] = jnp.zeros_like(own_ids)
    for pair in range(2):
        for lev in range(2):
            own_ids[pair, pl.ds(SIDE * lev, SIDE), pl.ds(0, SIDE)] = region[LEVELS[pair][lev]].astype(F32)
    block[:, pl.ds(TOKENS, 16), :] = jnp.zeros((TILES, 16, 128), F32)
    for pair in range(2):
        for slot in (3, 5, 6):
            halo_out[pair, slot, :, pl.ds(32, 8), :] = jnp.zeros((TILES, 8, 128), F32)
            back_out[pair, slot, :, pl.ds(32, 8), :] = jnp.zeros((TILES, 8, 128), F32)

    def id_copy(pair, side):
        rows, cols = ((0, 1), (1, 0), (1, 1))[side]
        sign = 1 if pair == 0 else -1
        return pltpu.make_async_remote_copy(
            src_ref=own_ids.at[pair],
            dst_ref=far_ids.at[pair, side],
            send_sem=id_send.at[pair, side],
            recv_sem=id_recv.at[pair, side],
            device_id=device(sign * rows, sign * cols),
            device_id_type=MESH,
        )

    def piece_copy(pair, slot, back):
        rows, cols = FROM[slot]
        sign = (1 if pair == 0 else -1) * (1 if back else -1)
        size = SLOT if slot in (0, 1, 2, 4) else 40
        source, target = (back_out, back_in) if back else (halo_out, halo_in)
        send, recv = (back_send, back_recv) if back else (halo_send, halo_recv)
        return pltpu.make_async_remote_copy(
            src_ref=source.at[pair, slot, :, pl.ds(0, size)],
            dst_ref=target.at[pair, slot, :, pl.ds(0, size)],
            send_sem=send.at[pair, slot],
            recv_sem=recv.at[pair, slot],
            device_id=device(sign * rows, sign * cols),
            device_id_type=MESH,
        )

    order = [slot for step in STEPS for slot in slots_of(step)]

    for tile in range(TILES):
        token_load(tile).wait()
    for load in loads:
        load.start()
    for pair, slot in order:
        for first, count, where in piece_runs(pair, slot):
            halo_out[pair, slot, :, pl.ds(first, count), :] = block[:, pl.ds(where, count), :]
    pl.semaphore_wait(barrier, len(around))
    for pair in range(2):
        for side in range(3):
            id_copy(pair, side).start()
    for pair, slot in order:
        piece_copy(pair, slot, False).start()

    ids[...] = own_ids[...]
    make_bias(rel_index, rel_table, table, bias)

    def all_ids():
        for pair in range(2):
            for side in range(3):
                id_copy(pair, side).wait()
            line = lax.broadcasted_iota(jnp.int32, (2 * SIDE, 128), 0) % SIDE
            lane = lax.broadcasted_iota(jnp.int32, (2 * SIDE, 128), 1)
            far_row = line >= SIDE - 3 if pair == 0 else line < 3
            far_col = lane >= SIDE - 6 if pair == 0 else lane < 6
            ids[pair] = jnp.where(
                far_row,
                jnp.where(far_col, far_ids[pair, 2], far_ids[pair, 1]),
                jnp.where(far_col, far_ids[pair, 0], own_ids[pair]),
            )

    for load in loads[:-1]:
        load.wait()

    def run(step, _):
        for number, windows in enumerate(STEPS):

            @pl.when(step == number)
            def _():
                if number == 1:
                    all_ids()
                for pair, slot in slots_of(windows):
                    piece_copy(pair, slot, False).wait_recv()
                for place, window in enumerate(windows):
                    for token, count, slot, first in segments(window):
                        at = pl.ds(place * WTOK + token, count)
                        if slot is None:
                            part[:, at, :] = block[:, pl.ds(first, count), :]
                        else:
                            part[:, at, :] = halo_in[window[0], slot, :, pl.ds(first, count), :]
                    mark_window(ids, marks, window, place * WTOK, lat, lat_count)

        for place in range(G):
            normed[pl.ds(place * WTOK, WTOK), :] = norm(
                wide(part, place * WTOK, WTOK), norm1_gain[...], norm1_bias[...]
            ).astype(BF16)
        for third in range(3):
            columns = pl.ds(512 * third, 512)
            packed = jnp.dot(normed[...], wq[:, columns], preferred_element_type=F32) + qkv_bias[columns].reshape(1, 512)
            if third == 0:
                packed = packed * 0.125
            qkv[:, columns] = packed.astype(BF16)
        for place in range(G):
            attend(qkv, attended, bias, marks, place * WTOK)
        hidden = jnp.dot(attended[...], wp[...], preferred_element_type=F32) + proj_bias[...] + wide(part, 0, ROWS)
        put_wide(part, 0, ROWS, hidden)
        normed[...] = norm(hidden, norm2_gain[...], norm2_bias[...]).astype(BF16)
        for quarter in range(4):
            columns = pl.ds(512 * quarter, 512)
            units = jnp.dot(normed[...], w1[:, columns], preferred_element_type=F32) + fc1_bias[:, columns]
            active[:, columns] = (0.5 * units * (1.0 + lax.erf(units * 0.7071067811865476))).astype(BF16)
        result = jnp.dot(active[...], w2[...], preferred_element_type=F32) + fc2_bias[...] + wide(part, 0, ROWS)
        put_wide(part, 0, ROWS, result)

        for number, windows in enumerate(STEPS):

            @pl.when(step == number)
            def _():
                for place, window in enumerate(windows):
                    for token, count, slot, first in segments(window):
                        at = pl.ds(place * WTOK + token, count)
                        if slot is None:
                            block[:, pl.ds(first, count), :] = part[:, at, :]
                        else:
                            back_out[window[0], slot, :, pl.ds(first, count), :] = part[:, at, :]
                for pair, slot in slots_of(windows):
                    piece_copy(pair, slot, True).start()

        return 0

    lax.fori_loop(0, len(STEPS), run, 0)

    def merge(pair):
        for other, slot in order:
            if other == pair:
                piece_copy(pair, slot, True).wait_recv()
                for first, count, where in piece_runs(pair, slot):
                    block[:, pl.ds(where, count), :] = back_in[pair, slot, :, pl.ds(first, count), :]
        if pair == 0:
            loads[-1].wait()

        def merge_norm(step, _):
            for number in range(4):
                at = step * 4 + number
                line = at + 12 if pair == 0 else lax.rem(at + 36, 48)
                values = jnp.concatenate(
                    [
                        block[tile, pl.ds(line * 2 * SIDE + row * SIDE + col, 16, stride=2), :]
                        for col in range(2)
                        for row in range(2)
                        for tile in range(TILES)
                    ],
                    1,
                )
                normed3[pl.ds(pl.multiple_of(at * 16, 16), 16), :] = norm(
                    values, merge_gain[...], merge_bias[...]
                ).astype(BF16)
            return 0

        lax.fori_loop(0, 6, merge_norm, 0)
        for quarter in range(4):
            merged = jnp.dot(normed3[...], wm[:, pl.ds(256 * quarter, 256)], preferred_element_type=F32)
            for at in range(24):
                for half in range(2):
                    product[
                        2 * quarter + half, pl.ds(at % 12 * 48 + LEVELS[pair][at // 12], 12, stride=4), :
                    ] = merged[16 * at : 16 * at + 12, 128 * half : 128 * (half + 1)]

    merge(0)
    merge(1)
    for tile in range(8):
        out[:, :, pl.ds(128 * tile, 128)] = product[tile].astype(BF16).reshape(144, 4, 128)

    for pair, slot in order:
        piece_copy(pair, slot, False).wait_send()
        piece_copy(pair, slot, True).wait_send()


def per_device(mesh_shape, tokens, region, rel_index, rel_table, *rest):
    (
        norm1_gain,
        norm1_bias,
        qkv_weight,
        qkv_bias,
        proj_weight,
        proj_bias,
        norm2_gain,
        norm2_bias,
        fc1_weight,
        fc1_bias,
        fc2_weight,
        fc2_bias,
        merge_gain,
        merge_bias,
        merge_weight,
    ) = rest
    lines = [
        value.reshape(1, -1)
        for value in (
            norm1_gain,
            norm1_bias,
            proj_bias,
            norm2_gain,
            norm2_bias,
            fc1_bias,
            fc2_bias,
            merge_gain,
            merge_bias,
        )
    ]
    lines.insert(2, qkv_bias)
    hbm = pl.BlockSpec(memory_space=pl.ANY)
    vmem = pl.BlockSpec(memory_space=pltpu.VMEM)
    merged = pl.pallas_call(
        functools.partial(kernel, *mesh_shape),
        out_shape=jax.ShapeDtypeStruct((144, 4, 1024), BF16),
        in_specs=[hbm] * 6 + [vmem] * 13,
        out_specs=vmem,
        scratch_shapes=[
            pltpu.VMEM((TILES, TOKENS + 16, 128), F32),
            pltpu.VMEM((TILES, ROWS, 128), F32),
            pltpu.VMEM((512, 1536), BF16),
            pltpu.VMEM((512, 512), BF16),
            pltpu.VMEM((512, 2048), BF16),
            pltpu.VMEM((2048, 512), BF16),
            pltpu.VMEM((2048, 1024), BF16),
            pltpu.VMEM((8, WTOK, WTOK), F32),
            pltpu.VMEM((ROWS, 128), BF16),
            pltpu.VMEM((ROWS, 512), BF16),
            pltpu.VMEM((ROWS, 1536), BF16),
            pltpu.VMEM((ROWS, 512), BF16),
            pltpu.VMEM((ROWS, 2048), BF16),
            pltpu.VMEM((384, 2048), BF16),
            pltpu.VMEM((8, 576, 128), F32),
            pltpu.VMEM((8, 768), F32),
            pltpu.VMEM((2, 2 * SIDE, 128), F32),
            pltpu.VMEM((2, 3, 2 * SIDE, 128), F32),
            pltpu.VMEM((2, 2 * SIDE, 128), F32),
        ]
        + [pltpu.VMEM((2, 7, TILES, SLOT, 128), F32)] * 4
        + [
            pltpu.SemaphoreType.DMA((TILES + 5,)),
            pltpu.SemaphoreType.DMA((2, 3)),
            pltpu.SemaphoreType.DMA((2, 3)),
        ]
        + [pltpu.SemaphoreType.DMA((2, 7))] * 4,
        compiler_params=pltpu.CompilerParams(
            collective_id=0, has_side_effects=True, vmem_limit_bytes=60 * 2**20
        ),
        name="block",
    )(
        tokens.reshape(TOKENS, 512),
        qkv_weight,
        proj_weight,
        fc1_weight,
        fc2_weight,
        merge_weight,
        region,
        rel_index,
        rel_table,
        *lines,
    )
    return merged.reshape(12, 12, 4, 1024).transpose(2, 0, 1, 3)


def solution(mesh):
    shape = (mesh.shape["lat"], mesh.shape["lon"])
    return jax.shard_map(
        functools.partial(per_device, shape),
        mesh=mesh,
        in_specs=(P(None, "lat", "lon", None), P(None, "lat", "lon")) + (P(),) * 17,
        out_specs=P(None, "lat", "lon", None),
        check_vma=False,
    )
```

```python
import functools

import jax
import jax.numpy as jnp
from jax import lax
from jax.experimental import pallas as pl
from jax.experimental.pallas import tpu as pltpu
from jax.sharding import PartitionSpec as P

MESH = pl.DeviceIdType.MESH
F32 = jnp.float32
BF16 = jnp.bfloat16
EPS = 1e-05
SIDE = 24
WTOK = 144
G = 4
ROWS = G * WTOK
TOKENS = 4 * SIDE * SIDE
TILES = 4
SLOT = 72

LEVELS = ((1, 2), (3, 0))
CORNER = ((-3, -6), (3, 6))
PIECES = (
    ((3, 6, 18, 6), (9, 6, 18, 6), (15, 6, 18, 6), (0, 3, 18, 6), (21, 3, 6, 12), (21, 3, 0, 6), (21, 3, 18, 6)),
    ((3, 6, 0, 6), (9, 6, 0, 6), (15, 6, 0, 6), (21, 3, 0, 6), (0, 3, 6, 12), (0, 3, 18, 6), (0, 3, 0, 6)),
)
FROM = ((0, -1), (0, -1), (0, -1), (0, -1), (-1, 0), (-1, 0), (-1, -1))
STEPS = (
    ((0, 1, 1), (0, 2, 1), (1, 0, 0), (1, 1, 0)),
    ((0, 1, 0), (0, 2, 0), (0, 3, 0), (1, 0, 1)),
    ((0, 0, 0), (0, 0, 1), (1, 3, 1), (1, 3, 0)),
    ((1, 1, 1), (1, 2, 1)),
    ((0, 3, 1), (1, 2, 0)),
)
LOOPED = 3


def segments(window):
    pair, wrow, wcol = window
    row0, col0 = CORNER[pair][0] + 6 * wrow, CORNER[pair][1] + 12 * wcol
    runs = []
    for lev in range(2):
        for row in range(6):
            for half in range(2):
                at_row, at_col = row0 + row, col0 + 6 * half
                where_row, where_col = at_row % SIDE, at_col % SIDE
                away = (at_row // SIDE, at_col // SIDE)
                token = (lev * 6 + row) * 12 + 6 * half
                if away == (0, 0):
                    slot, first = None, (LEVELS[pair][lev] * SIDE + where_row) * SIDE + where_col
                else:
                    slot = None
                    for number, (first_row, rows, first_col, cols) in enumerate(PIECES[pair]):
                        if first_row <= where_row < first_row + rows and first_col <= where_col < first_col + cols:
                            slot = number
                            first = (lev * rows + where_row - first_row) * cols + where_col - first_col
                if runs and runs[-1][2] == slot and runs[-1][0] + runs[-1][1] == token and runs[-1][3] + runs[-1][1] == first:
                    runs[-1] = (runs[-1][0], runs[-1][1] + 6, slot, runs[-1][3])
                else:
                    runs.append((token, 6, slot, first))
    return runs


def slots_of(windows):
    return [
        (window[0], slot)
        for window in windows
        for slot in sorted({run[2] for run in segments(window) if run[2] is not None})
    ]


def piece_runs(pair, slot):
    first_row, rows, first_col, cols = PIECES[pair][slot]
    for lev in range(2):
        for row in range(rows):
            yield (lev * rows + row) * cols, cols, (LEVELS[pair][lev] * SIDE + first_row + row) * SIDE + first_col


def norm(values, gain, shift):
    centred = values - jnp.mean(values, -1, keepdims=True)
    variance = jnp.mean(centred * centred, -1, keepdims=True)
    return centred * lax.rsqrt(variance + EPS) * gain + shift


def wide(ref, first, count):
    return jnp.concatenate([ref[tile, pl.ds(first, count), :] for tile in range(TILES)], 1)


def put_wide(ref, first, count, values):
    for tile in range(TILES):
        ref[tile, pl.ds(first, count), :] = values[:, 128 * tile : 128 * (tile + 1)]


def make_bias(rel_index, rel_table, table, bias):
    table[...] = jnp.zeros_like(table)
    table[:, pl.ds(0, rel_table.shape[1])] = rel_table[...]

    def rows_at(step, _):
        at = pl.multiple_of(step * 8, 8)
        for first, count in ((0, 128), (128, 16)):
            index = rel_index[pl.ds(at, 8), pl.ds(first, count)]
            if count < 128:
                index = jnp.concatenate([index, jnp.zeros((8, 128 - count), jnp.int32)], 1)
            low, high = index & 127, index >> 7
            for head in range(8):
                found = jnp.zeros((8, 128), F32)
                for part in range(6):
                    row = table[pl.ds(head, 1), pl.ds(128 * part, 128)]
                    drawn = jnp.take_along_axis(
                        jnp.broadcast_to(row, (8, 128)), low, axis=1, mode="promise_in_bounds"
                    )
                    found = jnp.where(high == part, drawn, found)
                bias[head, pl.ds(at, 8), pl.ds(first, count)] = found[:, :count]
        return 0

    lax.fori_loop(0, WTOK // 8, rows_at, 0)


def attend(qkv, attended, bias, marks, first):
    lane = lax.broadcasted_iota(jnp.int32, (1, 128), 1)
    left = lane < 64
    mark = marks[pl.ds(first, WTOK), :]
    barred = jnp.where(mark > 0, jnp.zeros_like(mark), jnp.full_like(mark, -1e30))
    ones = jnp.ones((WTOK, 128), BF16)
    for pair in range(4):
        query = qkv[pl.ds(first, WTOK), pl.ds(128 * pair, 128)]
        key = qkv[pl.ds(first, WTOK), pl.ds(512 + 128 * pair, 128)]
        value = qkv[pl.ds(first, WTOK), pl.ds(1024 + 128 * pair, 128)]
        keys = jnp.concatenate([key, barred], 1)
        values = jnp.concatenate([value, ones], 1)
        zero = jnp.zeros_like(query)
        results = []
        for side in range(2):
            part = jnp.where(left, query, zero) if side == 0 else jnp.where(left, zero, query)
            scores = lax.dot_general(
                jnp.concatenate([part, mark], 1), keys, (((1,), (1,)), ((), ())), preferred_element_type=F32
            )
            scores = scores + bias[2 * pair + side]
            powers = jnp.exp(scores - jnp.max(scores, -1, keepdims=True)).astype(BF16)
            total = jnp.dot(powers, values, preferred_element_type=F32)
            results.append(total[:, :128] / total[:, 128:])
        attended[pl.ds(first, WTOK), pl.ds(128 * pair, 128)] = jnp.where(left, results[0], results[1]).astype(BF16)


def spread(spots):
    token = lax.broadcasted_iota(jnp.int32, (WTOK, 128), 0)
    lev, row, col = token // 72, token // 12 % 6, token % 12
    spots[0] = lev * SIDE + row
    spots[1] = row
    spots[2] = col


def kinds(pair, regions, lat, lat_count):
    line = lax.broadcasted_iota(jnp.int32, (2 * SIDE, 128), 0)
    lev = jnp.where(line >= SIDE, 1, 0)
    row = line - SIDE * lev
    if pair == 0:
        row = jnp.where(row >= SIDE - 3, row - SIDE, row)
    else:
        row = jnp.where(row < 3, row + SIDE, row)
    whole = lat_count * SIDE
    orig = lat * SIDE + row
    orig = jnp.where(orig < 0, orig + whole, jnp.where(orig >= whole, orig - whole, orig))
    band = jnp.where(orig >= whole - 3, 1, 0)
    if pair == 1:
        band = band + 2 * lev
    return regions + (3 * band + 1).astype(F32)


def mark_window(ids, spots, marks, window, first):
    pair, wrow, wcol = window
    row0, col0 = CORNER[pair][0] + 6 * wrow, CORNER[pair][1] + 12 * wcol
    line, row, col = spots[0] + row0, spots[1], spots[2] + col0
    if row0 < 0:
        line = jnp.where(row < -row0, line + SIDE, line)
    elif row0 + 6 > SIDE:
        line = jnp.where(row >= SIDE - row0, line - SIDE, line)
    if col0 < 0:
        col = jnp.where(col < 0, col + SIDE, col)
    elif col0 + 12 > SIDE:
        col = jnp.where(col >= SIDE, col - SIDE, col)
    lane = lax.broadcasted_iota(jnp.int32, (WTOK, 128), 1)
    pick = jnp.where(lane == line, 1.0, 0.0).astype(BF16)
    rows = jnp.dot(pick, ids[pair].astype(BF16), preferred_element_type=F32)
    own = jnp.where(lane == col, rows, 0.0).astype(BF16)
    kind = jnp.dot(own, jnp.ones((128, 128), BF16), preferred_element_type=F32)
    marks[pl.ds(first, WTOK), :] = jnp.where(lane.astype(F32) + 1.0 == kind, 1.0, 0.0).astype(BF16)


def kernel(
    lat_count,
    lon_count,
    tokens,
    qkv_weight,
    proj_weight,
    fc1_weight,
    fc2_weight,
    merge_weight,
    region,
    rel_index,
    rel_table,
    norm1_gain,
    norm1_bias,
    qkv_bias,
    proj_bias,
    norm2_gain,
    norm2_bias,
    fc1_bias,
    fc2_bias,
    merge_gain,
    merge_bias,
    out,
    block,
    part,
    wq,
    wp,
    w1,
    w2,
    wm,
    bias,
    marks,
    normed,
    qkv,
    attended,
    active,
    normed3,
    product,
    table,
    own_ids,
    far_ids,
    ids,
    spots,
    halo_out,
    halo_in,
    back_out,
    back_in,
    load_sem,
    id_send,
    id_recv,
    halo_send,
    halo_recv,
    back_send,
    back_recv,
):
    lat, lon = lax.axis_index("lat"), lax.axis_index("lon")

    def device(rows, cols):
        return lax.rem(lat + rows + lat_count, lat_count), lax.rem(lon + cols + lon_count, lon_count)

    barrier = pltpu.get_barrier_semaphore()
    around = ((0, 1), (1, 0), (1, 1), (0, -1), (-1, 0), (-1, -1))
    for away in around:
        pl.semaphore_signal(barrier, inc=1, device_id=device(*away), device_id_type=MESH)

    def token_load(tile):
        return pltpu.make_async_copy(
            tokens.at[:, pl.ds(128 * tile, 128)], block.at[tile, pl.ds(0, TOKENS)], load_sem.at[tile]
        )

    for tile in range(TILES):
        token_load(tile).start()

    loads = [
        pltpu.make_async_copy(source, target, load_sem.at[TILES + number])
        for number, (source, target) in enumerate(
            ((qkv_weight, wq), (proj_weight, wp), (fc1_weight, w1), (fc2_weight, w2), (merge_weight, wm))
        )
    ]

    own_ids[...] = jnp.zeros_like(own_ids)
    for pair in range(2):
        for lev in range(2):
            own_ids[pair, pl.ds(SIDE * lev, SIDE), pl.ds(0, SIDE)] = region[LEVELS[pair][lev]].astype(F32)
    block[:, pl.ds(TOKENS, 16), :] = jnp.zeros((TILES, 16, 128), F32)
    for pair in range(2):
        for slot in (3, 5, 6):
            halo_out[pair, slot, :, pl.ds(32, 8), :] = jnp.zeros((TILES, 8, 128), F32)
            back_out[pair, slot, :, pl.ds(32, 8), :] = jnp.zeros((TILES, 8, 128), F32)

    def id_copy(pair, side):
        rows, cols = ((0, 1), (1, 0), (1, 1))[side]
        sign = 1 if pair == 0 else -1
        return pltpu.make_async_remote_copy(
            src_ref=own_ids.at[pair],
            dst_ref=far_ids.at[pair, side],
            send_sem=id_send.at[pair, side],
            recv_sem=id_recv.at[pair, side],
            device_id=device(sign * rows, sign * cols),
            device_id_type=MESH,
        )

    def piece_copy(pair, slot, back):
        rows, cols = FROM[slot]
        sign = (1 if pair == 0 else -1) * (1 if back else -1)
        size = SLOT if slot in (0, 1, 2, 4) else 40
        source, target = (back_out, back_in) if back else (halo_out, halo_in)
        send, recv = (back_send, back_recv) if back else (halo_send, halo_recv)
        return pltpu.make_async_remote_copy(
            src_ref=source.at[pair, slot, :, pl.ds(0, size)],
            dst_ref=target.at[pair, slot, :, pl.ds(0, size)],
            send_sem=send.at[pair, slot],
            recv_sem=recv.at[pair, slot],
            device_id=device(sign * rows, sign * cols),
            device_id_type=MESH,
        )

    order = [slot for step in STEPS for slot in slots_of(step)]
    late = slots_of(STEPS[LOOPED])

    for tile in range(TILES):
        token_load(tile).wait()
    for load in loads:
        load.start()
    for pair, slot in order:
        for first, count, where in piece_runs(pair, slot):
            halo_out[pair, slot, :, pl.ds(first, count), :] = block[:, pl.ds(where, count), :]
    pl.semaphore_wait(barrier, len(around))
    for pair in range(2):
        for side in range(3):
            id_copy(pair, side).start()
    for pair, slot in order:
        if (pair, slot) not in late:
            piece_copy(pair, slot, False).start()

    ids[...] = jnp.zeros_like(ids)
    for pair in range(2):
        ids[pair, pl.ds(0, 2 * SIDE), :] = kinds(pair, own_ids[pair], lat, lat_count)
    spread(spots)
    make_bias(rel_index, rel_table, table, bias)

    def all_ids():
        for pair in range(2):
            for side in range(3):
                id_copy(pair, side).wait()
            line = lax.broadcasted_iota(jnp.int32, (2 * SIDE, 128), 0)
            line = jnp.where(line >= SIDE, line - SIDE, line)
            lane = lax.broadcasted_iota(jnp.int32, (2 * SIDE, 128), 1)
            far_row = line >= SIDE - 3 if pair == 0 else line < 3
            far_col = lane >= SIDE - 6 if pair == 0 else lane < 6
            regions = jnp.where(
                far_row,
                jnp.where(far_col, far_ids[pair, 2], far_ids[pair, 1]),
                jnp.where(far_col, far_ids[pair, 0], own_ids[pair]),
            )
            ids[pair, pl.ds(0, 2 * SIDE), :] = kinds(pair, regions, lat, lat_count)

    for load in loads[:-1]:
        load.wait()

    def first_norm(first, count):
        for place in range(first, first + count):
            normed[pl.ds(place * WTOK, WTOK), :] = norm(
                wide(part, place * WTOK, WTOK), norm1_gain[...], norm1_bias[...]
            ).astype(BF16)

    def pack(first, count):
        at = pl.ds(first * WTOK, count * WTOK)
        for third in range(3):
            columns = pl.ds(512 * third, 512)
            packed = jnp.dot(normed[at, :], wq[:, columns], preferred_element_type=F32)
            packed = packed + qkv_bias[columns].reshape(1, 512)
            if third == 0:
                packed = packed * 0.125
            qkv[at, columns] = packed.astype(BF16)

    def project(first, count):
        first, count = first * WTOK, count * WTOK
        at = pl.ds(first, count)
        hidden = jnp.dot(attended[at, :], wp[...], preferred_element_type=F32) + proj_bias[...]
        hidden = hidden + wide(part, first, count)
        put_wide(part, first, count, hidden)
        normed[at, :] = norm(hidden, norm2_gain[...], norm2_bias[...]).astype(BF16)

    def expand(first, count, quarter):
        at = pl.ds(first * WTOK, count * WTOK)
        columns = pl.ds(512 * quarter, 512)
        units = jnp.dot(normed[at, :], w1[:, columns], preferred_element_type=F32) + fc1_bias[:, columns]
        active[at, columns] = (0.5 * units * (1.0 + lax.erf(units * 0.7071067811865476))).astype(BF16)

    def contract(first, count):
        first, count = first * WTOK, count * WTOK
        result = jnp.dot(active[pl.ds(first, count), :], w2[...], preferred_element_type=F32) + fc2_bias[...]
        put_wide(part, first, count, result + wide(part, first, count))

    def compute(count):
        first_norm(0, count)
        pack(0, count)
        half = count // 2 if count > 2 else count
        early = half + half // 2 if count > 2 else count
        for place in range(early):
            attend(qkv, attended, bias, marks, place * WTOK)
        project(0, half)
        for place in range(early, count):
            attend(qkv, attended, bias, marks, place * WTOK)
        for quarter in range(4):
            expand(0, half, quarter)
        if half < count:
            project(half, half)
        contract(0, half)
        if half < count:
            for quarter in range(4):
                expand(half, half, quarter)
            contract(half, half)

    def gather(number):
        windows = STEPS[number]
        if number == 1:
            for pair, slot in late:
                piece_copy(pair, slot, False).start()
            all_ids()
        for pair, slot in slots_of(windows):
            piece_copy(pair, slot, False).wait_recv()
        for place, window in enumerate(windows):
            for token, count, slot, first in segments(window):
                at = pl.ds(place * WTOK + token, count)
                if slot is None:
                    part[:, at, :] = block[:, pl.ds(first, count), :]
                else:
                    part[:, at, :] = halo_in[window[0], slot, :, pl.ds(first, count), :]
            mark_window(ids, spots, marks, window, place * WTOK)

    def settle(number):
        windows = STEPS[number]
        for place, window in enumerate(windows):
            for token, count, slot, first in segments(window):
                at = pl.ds(place * WTOK + token, count)
                if slot is not None:
                    back_out[window[0], slot, :, pl.ds(first, count), :] = part[:, at, :]
        for pair, slot in slots_of(windows):
            piece_copy(pair, slot, True).start()
        for place, window in enumerate(windows):
            for token, count, slot, first in segments(window):
                at = pl.ds(place * WTOK + token, count)
                if slot is None:
                    block[:, pl.ds(first, count), :] = part[:, at, :]

    def run(step, _):
        for number in range(LOOPED):
            pl.when(step == number)(functools.partial(gather, number))
        compute(G)
        for number in range(LOOPED):
            pl.when(step == number)(functools.partial(settle, number))
        return 0

    lax.fori_loop(0, LOOPED, run, 0)
    for number in range(LOOPED, len(STEPS)):
        gather(number)
        compute(len(STEPS[number]))
        settle(number)

    def merge(pair):
        for other, slot in order:
            if other == pair:
                piece_copy(pair, slot, True).wait_recv()
                for first, count, where in piece_runs(pair, slot):
                    block[:, pl.ds(where, count), :] = back_in[pair, slot, :, pl.ds(first, count), :]
        if pair == 0:
            loads[-1].wait()

        def merge_norm(step, _):
            for number in range(8):
                at = step * 8 + number
                line = at + 12 if pair == 0 else lax.rem(at + 36, 48)
                values = jnp.concatenate(
                    [
                        block[tile, pl.ds(line * 2 * SIDE + row * SIDE + col, 16, stride=2), :]
                        for col in range(2)
                        for row in range(2)
                        for tile in range(TILES)
                    ],
                    1,
                )
                normed3[pl.ds(pl.multiple_of(at * 16, 16), 16), :] = norm(
                    values, merge_gain[...], merge_bias[...]
                ).astype(BF16)
            return 0

        lax.fori_loop(0, 3, merge_norm, 0)
        for quarter in range(4):
            merged = jnp.dot(normed3[...], wm[:, pl.ds(256 * quarter, 256)], preferred_element_type=F32)
            for at in range(24):
                for half in range(2):
                    product[
                        2 * quarter + half, pl.ds(at % 12 * 48 + LEVELS[pair][at // 12], 12, stride=4), :
                    ] = merged[16 * at : 16 * at + 12, 128 * half : 128 * (half + 1)]

    merge(0)
    merge(1)
    for tile in range(8):
        out[:, :, pl.ds(128 * tile, 128)] = product[tile].astype(BF16).reshape(144, 4, 128)

    for pair, slot in order:
        piece_copy(pair, slot, False).wait_send()
        piece_copy(pair, slot, True).wait_send()


def per_device(mesh_shape, tokens, region, rel_index, rel_table, *rest):
    (
        norm1_gain,
        norm1_bias,
        qkv_weight,
        qkv_bias,
        proj_weight,
        proj_bias,
        norm2_gain,
        norm2_bias,
        fc1_weight,
        fc1_bias,
        fc2_weight,
        fc2_bias,
        merge_gain,
        merge_bias,
        merge_weight,
    ) = rest
    lines = [
        value.reshape(1, -1)
        for value in (
            norm1_gain,
            norm1_bias,
            proj_bias,
            norm2_gain,
            norm2_bias,
            fc1_bias,
            fc2_bias,
            merge_gain,
            merge_bias,
        )
    ]
    lines.insert(2, qkv_bias)
    hbm = pl.BlockSpec(memory_space=pl.ANY)
    vmem = pl.BlockSpec(memory_space=pltpu.VMEM)
    merged = pl.pallas_call(
        functools.partial(kernel, *mesh_shape),
        out_shape=pltpu.VMEM((144, 4, 1024), BF16),
        in_specs=[hbm] * 6 + [vmem] * 13,
        out_specs=vmem,
        scratch_shapes=[
            pltpu.VMEM((TILES, TOKENS + 16, 128), F32),
            pltpu.VMEM((TILES, ROWS, 128), F32),
            pltpu.VMEM((512, 1536), BF16),
            pltpu.VMEM((512, 512), BF16),
            pltpu.VMEM((512, 2048), BF16),
            pltpu.VMEM((2048, 512), BF16),
            pltpu.VMEM((2048, 1024), BF16),
            pltpu.VMEM((8, WTOK, WTOK), F32),
            pltpu.VMEM((ROWS, 128), BF16),
            pltpu.VMEM((ROWS, 512), BF16),
            pltpu.VMEM((ROWS, 1536), BF16),
            pltpu.VMEM((ROWS, 512), BF16),
            pltpu.VMEM((ROWS, 2048), BF16),
            pltpu.VMEM((384, 2048), BF16),
            pltpu.VMEM((8, 576, 128), F32),
            pltpu.VMEM((8, 768), F32),
            pltpu.VMEM((2, 2 * SIDE, 128), F32),
            pltpu.VMEM((2, 3, 2 * SIDE, 128), F32),
            pltpu.VMEM((2, 128, 128), F32),
            pltpu.VMEM((3, WTOK, 128), jnp.int32),
        ]
        + [pltpu.VMEM((2, 7, TILES, SLOT, 128), F32)] * 4
        + [
            pltpu.SemaphoreType.DMA((TILES + 5,)),
            pltpu.SemaphoreType.DMA((2, 3)),
            pltpu.SemaphoreType.DMA((2, 3)),
        ]
        + [pltpu.SemaphoreType.DMA((2, 7))] * 4,
        compiler_params=pltpu.CompilerParams(
            collective_id=0, has_side_effects=True, vmem_limit_bytes=60 * 2**20
        ),
        name="block",
    )(
        tokens.reshape(TOKENS, 512),
        qkv_weight,
        proj_weight,
        fc1_weight,
        fc2_weight,
        merge_weight,
        region,
        rel_index,
        rel_table,
        *lines,
    )
    return merged.reshape(12, 12, 4, 1024).transpose(2, 0, 1, 3)


def solution(mesh):
    shape = (mesh.shape["lat"], mesh.shape["lon"])
    return jax.shard_map(
        functools.partial(per_device, shape),
        mesh=mesh,
        in_specs=(P(None, "lat", "lon", None), P(None, "lat", "lon")) + (P(),) * 17,
        out_specs=P(None, "lat", "lon", None),
        check_vma=False,
    )
```

```python
import functools

import jax
import jax.numpy as jnp
from jax import lax
from jax.experimental import pallas as pl
from jax.experimental.pallas import tpu as pltpu
from jax.sharding import PartitionSpec as P

MESH = pl.DeviceIdType.MESH
F32 = jnp.float32
BF16 = jnp.bfloat16
EPS = 1e-05
SIDE = 24
WTOK = 144
G = 4
ROWS = G * WTOK
TOKENS = 4 * SIDE * SIDE
TILES = 4
SLOT = 72

LEVELS = ((1, 2), (3, 0))
CORNER = ((-3, -6), (3, 6))
PIECES = (
    ((3, 6, 18, 6), (9, 6, 18, 6), (15, 6, 18, 6), (0, 3, 18, 6), (21, 3, 6, 12), (21, 3, 0, 6), (21, 3, 18, 6)),
    ((3, 6, 0, 6), (9, 6, 0, 6), (15, 6, 0, 6), (21, 3, 0, 6), (0, 3, 6, 12), (0, 3, 18, 6), (0, 3, 0, 6)),
)
FROM = ((0, -1), (0, -1), (0, -1), (0, -1), (-1, 0), (-1, 0), (-1, -1))
STEPS = (
    ((0, 1, 1), (0, 2, 1), (1, 0, 0), (1, 1, 0)),
    ((0, 1, 0), (0, 2, 0), (0, 3, 0), (1, 0, 1)),
    ((1, 1, 1), (1, 2, 1)),
    ((0, 0, 0), (0, 0, 1), (1, 3, 1), (1, 3, 0)),
    ((0, 3, 1), (1, 2, 0)),
)
LOOPED = (0, 1, 3)
BETWEEN, LAST = 2, 4
LINES = (tuple(range(2, 10)), (0, 1, 10, 11))


def segments(window):
    pair, wrow, wcol = window
    row0, col0 = CORNER[pair][0] + 6 * wrow, CORNER[pair][1] + 12 * wcol
    runs = []
    for lev in range(2):
        for row in range(6):
            for half in range(2):
                at_row, at_col = row0 + row, col0 + 6 * half
                where_row, where_col = at_row % SIDE, at_col % SIDE
                away = (at_row // SIDE, at_col // SIDE)
                token = (lev * 6 + row) * 12 + 6 * half
                if away == (0, 0):
                    slot, first = None, (LEVELS[pair][lev] * SIDE + where_row) * SIDE + where_col
                else:
                    slot = None
                    for number, (first_row, rows, first_col, cols) in enumerate(PIECES[pair]):
                        if first_row <= where_row < first_row + rows and first_col <= where_col < first_col + cols:
                            slot = number
                            first = (lev * rows + where_row - first_row) * cols + where_col - first_col
                if runs and runs[-1][2] == slot and runs[-1][0] + runs[-1][1] == token and runs[-1][3] + runs[-1][1] == first:
                    runs[-1] = (runs[-1][0], runs[-1][1] + 6, slot, runs[-1][3])
                else:
                    runs.append((token, 6, slot, first))
    return runs


def slots_of(windows):
    return [
        (window[0], slot)
        for window in windows
        for slot in sorted({run[2] for run in segments(window) if run[2] is not None})
    ]


def piece_runs(pair, slot):
    first_row, rows, first_col, cols = PIECES[pair][slot]
    for lev in range(2):
        for row in range(rows):
            yield (lev * rows + row) * cols, cols, (LEVELS[pair][lev] * SIDE + first_row + row) * SIDE + first_col


def norm(values, gain, shift):
    centred = values - jnp.mean(values, -1, keepdims=True)
    variance = jnp.mean(centred * centred, -1, keepdims=True)
    return centred * lax.rsqrt(variance + EPS) * gain + shift


def wide(ref, first, count):
    return jnp.concatenate([ref[tile, pl.ds(first, count), :] for tile in range(TILES)], 1)


def put_wide(ref, first, count, values):
    for tile in range(TILES):
        ref[tile, pl.ds(first, count), :] = values[:, 128 * tile : 128 * (tile + 1)]


def make_bias(rel_index, rel_table, table, bias):
    table[...] = jnp.zeros_like(table)
    table[:, pl.ds(0, rel_table.shape[1])] = rel_table[...]

    def rows_at(step, _):
        at = pl.multiple_of(step * 8, 8)
        for first, count in ((0, 128), (128, 16)):
            index = rel_index[pl.ds(at, 8), pl.ds(first, count)]
            if count < 128:
                index = jnp.concatenate([index, jnp.zeros((8, 128 - count), jnp.int32)], 1)
            low, high = index & 127, index >> 7
            for head in range(8):
                found = jnp.zeros((8, 128), F32)
                for part in range(6):
                    row = table[pl.ds(head, 1), pl.ds(128 * part, 128)]
                    drawn = jnp.take_along_axis(
                        jnp.broadcast_to(row, (8, 128)), low, axis=1, mode="promise_in_bounds"
                    )
                    found = jnp.where(high == part, drawn, found)
                bias[head, pl.ds(at, 8), pl.ds(first, count)] = found[:, :count]
        return 0

    lax.fori_loop(0, WTOK // 8, rows_at, 0)


def attend(qkv, attended, bias, marks, first):
    lane = lax.broadcasted_iota(jnp.int32, (1, 128), 1)
    left = lane < 64
    mark = marks[pl.ds(first, WTOK), :]
    barred = jnp.where(mark > 0, jnp.zeros_like(mark), jnp.full_like(mark, -1e30))
    ones = jnp.ones((WTOK, 128), BF16)
    for pair in range(4):
        query = qkv[pl.ds(first, WTOK), pl.ds(128 * pair, 128)]
        key = qkv[pl.ds(first, WTOK), pl.ds(512 + 128 * pair, 128)]
        value = qkv[pl.ds(first, WTOK), pl.ds(1024 + 128 * pair, 128)]
        keys = jnp.concatenate([key, barred], 1)
        values = jnp.concatenate([value, ones], 1)
        zero = jnp.zeros_like(query)
        results = []
        for side in range(2):
            part = jnp.where(left, query, zero) if side == 0 else jnp.where(left, zero, query)
            scores = lax.dot_general(
                jnp.concatenate([part, mark], 1), keys, (((1,), (1,)), ((), ())), preferred_element_type=F32
            )
            scores = scores + bias[2 * pair + side]
            powers = jnp.exp(scores - jnp.max(scores, -1, keepdims=True)).astype(BF16)
            total = jnp.dot(powers, values, preferred_element_type=F32)
            results.append(total[:, :128] / total[:, 128:])
        attended[pl.ds(first, WTOK), pl.ds(128 * pair, 128)] = jnp.where(left, results[0], results[1]).astype(BF16)


def spread(spots):
    token = lax.broadcasted_iota(jnp.int32, (WTOK, 128), 0)
    lev, row, col = token // 72, token // 12 % 6, token % 12
    spots[0] = lev * SIDE + row
    spots[1] = row
    spots[2] = col


def kinds(pair, regions, lat, lat_count):
    line = lax.broadcasted_iota(jnp.int32, (2 * SIDE, 128), 0)
    lev = jnp.where(line >= SIDE, 1, 0)
    row = line - SIDE * lev
    if pair == 0:
        row = jnp.where(row >= SIDE - 3, row - SIDE, row)
    else:
        row = jnp.where(row < 3, row + SIDE, row)
    whole = lat_count * SIDE
    orig = lat * SIDE + row
    orig = jnp.where(orig < 0, orig + whole, jnp.where(orig >= whole, orig - whole, orig))
    band = jnp.where(orig >= whole - 3, 1, 0)
    if pair == 1:
        band = band + 2 * lev
    return regions + (3 * band + 1).astype(F32)


def mark_window(ids, spots, marks, window, first):
    pair, wrow, wcol = window
    row0, col0 = CORNER[pair][0] + 6 * wrow, CORNER[pair][1] + 12 * wcol
    line, row, col = spots[0] + row0, spots[1], spots[2] + col0
    if row0 < 0:
        line = jnp.where(row < -row0, line + SIDE, line)
    elif row0 + 6 > SIDE:
        line = jnp.where(row >= SIDE - row0, line - SIDE, line)
    if col0 < 0:
        col = jnp.where(col < 0, col + SIDE, col)
    elif col0 + 12 > SIDE:
        col = jnp.where(col >= SIDE, col - SIDE, col)
    lane = lax.broadcasted_iota(jnp.int32, (WTOK, 128), 1)
    pick = jnp.where(lane == line, 1.0, 0.0).astype(BF16)
    rows = jnp.dot(pick, ids[pair].astype(BF16), preferred_element_type=F32)
    own = jnp.where(lane == col, rows, 0.0).astype(BF16)
    kind = jnp.dot(own, jnp.ones((128, 128), BF16), preferred_element_type=F32)
    marks[pl.ds(first, WTOK), :] = jnp.where(lane.astype(F32) + 1.0 == kind, 1.0, 0.0).astype(BF16)


def kernel(
    lat_count,
    lon_count,
    tokens,
    qkv_weight,
    proj_weight,
    fc1_weight,
    fc2_weight,
    merge_weight,
    region,
    rel_index,
    rel_table,
    norm1_gain,
    norm1_bias,
    qkv_bias,
    proj_bias,
    norm2_gain,
    norm2_bias,
    fc1_bias,
    fc2_bias,
    merge_gain,
    merge_bias,
    out,
    block,
    part,
    wq,
    wp,
    w1,
    w2,
    wm,
    bias,
    marks,
    normed,
    qkv,
    attended,
    active,
    normed3,
    product,
    table,
    own_ids,
    far_ids,
    ids,
    spots,
    halo_out,
    halo_in,
    back_out,
    back_in,
    load_sem,
    id_send,
    id_recv,
    halo_send,
    halo_recv,
    back_send,
    back_recv,
):
    lat, lon = lax.axis_index("lat"), lax.axis_index("lon")

    def device(rows, cols):
        return lax.rem(lat + rows + lat_count, lat_count), lax.rem(lon + cols + lon_count, lon_count)

    barrier = pltpu.get_barrier_semaphore()
    around = ((0, 1), (1, 0), (1, 1), (0, -1), (-1, 0), (-1, -1))
    for away in around:
        pl.semaphore_signal(barrier, inc=1, device_id=device(*away), device_id_type=MESH)

    def token_load(tile):
        return pltpu.make_async_copy(
            tokens.at[:, pl.ds(128 * tile, 128)], block.at[tile, pl.ds(0, TOKENS)], load_sem.at[tile]
        )

    for tile in range(TILES):
        token_load(tile).start()

    loads = [
        pltpu.make_async_copy(source, target, load_sem.at[TILES + number])
        for number, (source, target) in enumerate(
            ((qkv_weight, wq), (proj_weight, wp), (fc1_weight, w1), (fc2_weight, w2), (merge_weight, wm))
        )
    ]

    own_ids[...] = jnp.zeros_like(own_ids)
    for pair in range(2):
        for lev in range(2):
            own_ids[pair, pl.ds(SIDE * lev, SIDE), pl.ds(0, SIDE)] = region[LEVELS[pair][lev]].astype(F32)
    block[:, pl.ds(TOKENS, 16), :] = jnp.zeros((TILES, 16, 128), F32)
    for pair in range(2):
        for slot in (3, 5, 6):
            halo_out[pair, slot, :, pl.ds(32, 8), :] = jnp.zeros((TILES, 8, 128), F32)
            back_out[pair, slot, :, pl.ds(32, 8), :] = jnp.zeros((TILES, 8, 128), F32)

    def id_copy(pair, side):
        rows, cols = ((0, 1), (1, 0), (1, 1))[side]
        sign = 1 if pair == 0 else -1
        return pltpu.make_async_remote_copy(
            src_ref=own_ids.at[pair],
            dst_ref=far_ids.at[pair, side],
            send_sem=id_send.at[pair, side],
            recv_sem=id_recv.at[pair, side],
            device_id=device(sign * rows, sign * cols),
            device_id_type=MESH,
        )

    def piece_copy(pair, slot, back):
        rows, cols = FROM[slot]
        sign = (1 if pair == 0 else -1) * (1 if back else -1)
        size = SLOT if slot in (0, 1, 2, 4) else 40
        source, target = (back_out, back_in) if back else (halo_out, halo_in)
        send, recv = (back_send, back_recv) if back else (halo_send, halo_recv)
        return pltpu.make_async_remote_copy(
            src_ref=source.at[pair, slot, :, pl.ds(0, size)],
            dst_ref=target.at[pair, slot, :, pl.ds(0, size)],
            send_sem=send.at[pair, slot],
            recv_sem=recv.at[pair, slot],
            device_id=device(sign * rows, sign * cols),
            device_id_type=MESH,
        )

    order = [slot for step in STEPS for slot in slots_of(step)]
    late = slots_of(STEPS[BETWEEN])

    for tile in range(TILES):
        token_load(tile).wait()
    for load in loads:
        load.start()
    for pair, slot in order:
        for first, count, where in piece_runs(pair, slot):
            halo_out[pair, slot, :, pl.ds(first, count), :] = block[:, pl.ds(where, count), :]
    pl.semaphore_wait(barrier, len(around))
    for pair in range(2):
        for side in range(3):
            id_copy(pair, side).start()
    for pair, slot in order:
        if (pair, slot) not in late:
            piece_copy(pair, slot, False).start()

    ids[...] = jnp.zeros_like(ids)
    for pair in range(2):
        ids[pair, pl.ds(0, 2 * SIDE), :] = kinds(pair, own_ids[pair], lat, lat_count)
    spread(spots)
    make_bias(rel_index, rel_table, table, bias)

    def all_ids():
        for pair in range(2):
            for side in range(3):
                id_copy(pair, side).wait()
            line = lax.broadcasted_iota(jnp.int32, (2 * SIDE, 128), 0)
            line = jnp.where(line >= SIDE, line - SIDE, line)
            lane = lax.broadcasted_iota(jnp.int32, (2 * SIDE, 128), 1)
            far_row = line >= SIDE - 3 if pair == 0 else line < 3
            far_col = lane >= SIDE - 6 if pair == 0 else lane < 6
            regions = jnp.where(
                far_row,
                jnp.where(far_col, far_ids[pair, 2], far_ids[pair, 1]),
                jnp.where(far_col, far_ids[pair, 0], own_ids[pair]),
            )
            ids[pair, pl.ds(0, 2 * SIDE), :] = kinds(pair, regions, lat, lat_count)

    for load in loads[:-1]:
        load.wait()

    def first_norm(first, count):
        for place in range(first, first + count):
            normed[pl.ds(place * WTOK, WTOK), :] = norm(
                wide(part, place * WTOK, WTOK), norm1_gain[...], norm1_bias[...]
            ).astype(BF16)

    def pack(first, count):
        at = pl.ds(first * WTOK, count * WTOK)
        for third in range(3):
            columns = pl.ds(512 * third, 512)
            packed = jnp.dot(normed[at, :], wq[:, columns], preferred_element_type=F32)
            packed = packed + qkv_bias[columns].reshape(1, 512)
            if third == 0:
                packed = packed * 0.125
            qkv[at, columns] = packed.astype(BF16)

    def project(first, count):
        first, count = first * WTOK, count * WTOK
        at = pl.ds(first, count)
        hidden = jnp.dot(attended[at, :], wp[...], preferred_element_type=F32) + proj_bias[...]
        hidden = hidden + wide(part, first, count)
        put_wide(part, first, count, hidden)
        normed[at, :] = norm(hidden, norm2_gain[...], norm2_bias[...]).astype(BF16)

    def expand(first, count, quarter):
        at = pl.ds(first * WTOK, count * WTOK)
        columns = pl.ds(512 * quarter, 512)
        units = jnp.dot(normed[at, :], w1[:, columns], preferred_element_type=F32) + fc1_bias[:, columns]
        active[at, columns] = (0.5 * units * (1.0 + lax.erf(units * 0.7071067811865476))).astype(BF16)

    def contract(first, count):
        first, count = first * WTOK, count * WTOK
        result = jnp.dot(active[pl.ds(first, count), :], w2[...], preferred_element_type=F32) + fc2_bias[...]
        put_wide(part, first, count, result + wide(part, first, count))

    def compute(count):
        first_norm(0, count)
        pack(0, count)
        half = count // 2 if count > 2 else count
        early = half + half // 2 if count > 2 else count
        for place in range(early):
            attend(qkv, attended, bias, marks, place * WTOK)
        project(0, half)
        for place in range(early, count):
            attend(qkv, attended, bias, marks, place * WTOK)
        for quarter in range(4):
            expand(0, half, quarter)
        if half < count:
            project(half, half)
        contract(0, half)
        if half < count:
            for quarter in range(4):
                expand(half, half, quarter)
            contract(half, half)

    def gather(number):
        windows = STEPS[number]
        if number == 1:
            for pair, slot in late:
                piece_copy(pair, slot, False).start()
            all_ids()
        for pair, slot in slots_of(windows):
            piece_copy(pair, slot, False).wait_recv()
        for place, window in enumerate(windows):
            for token, count, slot, first in segments(window):
                at = pl.ds(place * WTOK + token, count)
                if slot is None:
                    part[:, at, :] = block[:, pl.ds(first, count), :]
                else:
                    part[:, at, :] = halo_in[window[0], slot, :, pl.ds(first, count), :]
            mark_window(ids, spots, marks, window, place * WTOK)

    def settle(number):
        windows = STEPS[number]
        for place, window in enumerate(windows):
            for token, count, slot, first in segments(window):
                at = pl.ds(place * WTOK + token, count)
                if slot is not None:
                    back_out[window[0], slot, :, pl.ds(first, count), :] = part[:, at, :]
        for pair, slot in slots_of(windows):
            piece_copy(pair, slot, True).start()
        for place, window in enumerate(windows):
            for token, count, slot, first in segments(window):
                at = pl.ds(place * WTOK + token, count)
                if slot is None:
                    block[:, pl.ds(first, count), :] = part[:, at, :]

    def short(number):
        gather(number)
        compute(len(STEPS[number]))
        settle(number)

    def run(step, _):
        for at, number in enumerate(LOOPED):
            if at == 2:
                pl.when(step == at)(functools.partial(short, BETWEEN))
            pl.when(step == at)(functools.partial(gather, number))
        compute(G)
        for at, number in enumerate(LOOPED):
            pl.when(step == at)(functools.partial(settle, number))
        return 0

    lax.fori_loop(0, len(LOOPED), run, 0)
    short(LAST)

    def merge(part_of, rows):
        for pair, slot in order:
            if (slot > 2) == (part_of == 1):
                piece_copy(pair, slot, True).wait_recv()
                for first, count, where in piece_runs(pair, slot):
                    block[:, pl.ds(where, count), :] = back_in[pair, slot, :, pl.ds(first, count), :]
        if part_of == 0:
            loads[-1].wait()
        levels = 8 // len(rows)

        def merge_norm(step, _):
            for number in range(8):
                at = step * 8 + number
                line = (step * levels + number // len(rows)) * 12 + rows[number % len(rows)]
                values = jnp.concatenate(
                    [
                        block[tile, pl.ds(line * 2 * SIDE + row * SIDE + col, 16, stride=2), :]
                        for col in range(2)
                        for row in range(2)
                        for tile in range(TILES)
                    ],
                    1,
                )
                normed3[pl.ds(pl.multiple_of(at * 16, 16), 16), :] = norm(
                    values, merge_gain[...], merge_bias[...]
                ).astype(BF16)
            return 0

        lax.fori_loop(0, 4 // levels, merge_norm, 0)
        for quarter in range(4):
            merged = jnp.dot(
                normed3[pl.ds(0, 64 * len(rows)), :],
                wm[:, pl.ds(256 * quarter, 256)],
                preferred_element_type=F32,
            )
            for at in range(4 * len(rows)):
                first = rows[at % len(rows)] * 48 + at // len(rows)
                for half in range(2):
                    product[2 * quarter + half, pl.ds(first, 12, stride=4), :] = merged[
                        16 * at : 16 * at + 12, 128 * half : 128 * (half + 1)
                    ]

    for part_of, rows in enumerate(LINES):
        merge(part_of, rows)
    for tile in range(8):
        out[:, :, pl.ds(128 * tile, 128)] = product[tile].astype(BF16).reshape(144, 4, 128)

    for pair, slot in order:
        piece_copy(pair, slot, False).wait_send()
        piece_copy(pair, slot, True).wait_send()


def per_device(mesh_shape, tokens, region, rel_index, rel_table, *rest):
    (
        norm1_gain,
        norm1_bias,
        qkv_weight,
        qkv_bias,
        proj_weight,
        proj_bias,
        norm2_gain,
        norm2_bias,
        fc1_weight,
        fc1_bias,
        fc2_weight,
        fc2_bias,
        merge_gain,
        merge_bias,
        merge_weight,
    ) = rest
    lines = [
        value.reshape(1, -1)
        for value in (
            norm1_gain,
            norm1_bias,
            proj_bias,
            norm2_gain,
            norm2_bias,
            fc1_bias,
            fc2_bias,
            merge_gain,
            merge_bias,
        )
    ]
    lines.insert(2, qkv_bias)
    hbm = pl.BlockSpec(memory_space=pl.ANY)
    vmem = pl.BlockSpec(memory_space=pltpu.VMEM)
    merged = pl.pallas_call(
        functools.partial(kernel, *mesh_shape),
        out_shape=pltpu.VMEM((144, 4, 1024), BF16),
        in_specs=[hbm] * 6 + [vmem] * 13,
        out_specs=vmem,
        scratch_shapes=[
            pltpu.VMEM((TILES, TOKENS + 16, 128), F32),
            pltpu.VMEM((TILES, ROWS, 128), F32),
            pltpu.VMEM((512, 1536), BF16),
            pltpu.VMEM((512, 512), BF16),
            pltpu.VMEM((512, 2048), BF16),
            pltpu.VMEM((2048, 512), BF16),
            pltpu.VMEM((2048, 1024), BF16),
            pltpu.VMEM((8, WTOK, WTOK), F32),
            pltpu.VMEM((ROWS, 128), BF16),
            pltpu.VMEM((ROWS, 512), BF16),
            pltpu.VMEM((ROWS, 1536), BF16),
            pltpu.VMEM((ROWS, 512), BF16),
            pltpu.VMEM((ROWS, 2048), BF16),
            pltpu.VMEM((512, 2048), BF16),
            pltpu.VMEM((8, 576, 128), F32),
            pltpu.VMEM((8, 768), F32),
            pltpu.VMEM((2, 2 * SIDE, 128), F32),
            pltpu.VMEM((2, 3, 2 * SIDE, 128), F32),
            pltpu.VMEM((2, 128, 128), F32),
            pltpu.VMEM((3, WTOK, 128), jnp.int32),
        ]
        + [pltpu.VMEM((2, 7, TILES, SLOT, 128), F32)] * 4
        + [
            pltpu.SemaphoreType.DMA((TILES + 5,)),
            pltpu.SemaphoreType.DMA((2, 3)),
            pltpu.SemaphoreType.DMA((2, 3)),
        ]
        + [pltpu.SemaphoreType.DMA((2, 7))] * 4,
        compiler_params=pltpu.CompilerParams(
            collective_id=0, has_side_effects=True, vmem_limit_bytes=60 * 2**20
        ),
        name="block",
    )(
        tokens.reshape(TOKENS, 512),
        qkv_weight,
        proj_weight,
        fc1_weight,
        fc2_weight,
        merge_weight,
        region,
        rel_index,
        rel_table,
        *lines,
    )
    return merged.reshape(12, 12, 4, 1024).transpose(2, 0, 1, 3)


def solution(mesh):
    shape = (mesh.shape["lat"], mesh.shape["lon"])
    return jax.shard_map(
        functools.partial(per_device, shape),
        mesh=mesh,
        in_specs=(P(None, "lat", "lon", None), P(None, "lat", "lon")) + (P(),) * 17,
        out_specs=P(None, "lat", "lon", None),
        check_vma=False,
    )
```

```python
import functools

import jax
import jax.numpy as jnp
from jax import lax
from jax.experimental import pallas as pl
from jax.experimental.pallas import tpu as pltpu
from jax.sharding import PartitionSpec as P

MESH = pl.DeviceIdType.MESH
F32 = jnp.float32
BF16 = jnp.bfloat16
EPS = 1e-05
SIDE = 24
WTOK = 144
G = 4
ROWS = G * WTOK
TOKENS = 4 * SIDE * SIDE
TILES = 4
SLOT = 72

LEVELS = ((1, 2), (3, 0))
CORNER = ((-3, -6), (3, 6))
PIECES = (
    ((3, 6, 18, 6), (9, 6, 18, 6), (15, 6, 18, 6), (0, 3, 18, 6), (21, 3, 6, 12), (21, 3, 0, 6), (21, 3, 18, 6)),
    ((3, 6, 0, 6), (9, 6, 0, 6), (15, 6, 0, 6), (21, 3, 0, 6), (0, 3, 6, 12), (0, 3, 18, 6), (0, 3, 0, 6)),
)
FROM = ((0, -1), (0, -1), (0, -1), (0, -1), (-1, 0), (-1, 0), (-1, -1))
STEPS = (
    ((0, 1, 1), (0, 2, 1), (1, 0, 0), (1, 1, 0)),
    ((0, 1, 0), (0, 2, 0), (0, 3, 0), (1, 0, 1)),
    ((1, 1, 1), (1, 2, 1)),
    ((0, 0, 0), (0, 0, 1), (1, 3, 1), (1, 3, 0)),
    ((0, 3, 1), (1, 2, 0)),
)
LOOPED = (0, 1, 3)
BETWEEN, LAST = 2, 4
LINES = (tuple(range(2, 10)), (0, 1, 10, 11))


def segments(window):
    pair, wrow, wcol = window
    row0, col0 = CORNER[pair][0] + 6 * wrow, CORNER[pair][1] + 12 * wcol
    runs = []
    for lev in range(2):
        for row in range(6):
            for half in range(2):
                at_row, at_col = row0 + row, col0 + 6 * half
                where_row, where_col = at_row % SIDE, at_col % SIDE
                away = (at_row // SIDE, at_col // SIDE)
                token = (lev * 6 + row) * 12 + 6 * half
                if away == (0, 0):
                    slot, first = None, (LEVELS[pair][lev] * SIDE + where_row) * SIDE + where_col
                else:
                    slot = None
                    for number, (first_row, rows, first_col, cols) in enumerate(PIECES[pair]):
                        if first_row <= where_row < first_row + rows and first_col <= where_col < first_col + cols:
                            slot = number
                            first = (lev * rows + where_row - first_row) * cols + where_col - first_col
                if runs and runs[-1][2] == slot and runs[-1][0] + runs[-1][1] == token and runs[-1][3] + runs[-1][1] == first:
                    runs[-1] = (runs[-1][0], runs[-1][1] + 6, slot, runs[-1][3])
                else:
                    runs.append((token, 6, slot, first))
    return runs


def slots_of(windows):
    return [
        (window[0], slot)
        for window in windows
        for slot in sorted({run[2] for run in segments(window) if run[2] is not None})
    ]


def piece_runs(pair, slot):
    first_row, rows, first_col, cols = PIECES[pair][slot]
    for lev in range(2):
        for row in range(rows):
            yield (lev * rows + row) * cols, cols, (LEVELS[pair][lev] * SIDE + first_row + row) * SIDE + first_col


def norm(values, gain, shift):
    centred = values - jnp.mean(values, -1, keepdims=True)
    variance = jnp.mean(centred * centred, -1, keepdims=True)
    return centred * lax.rsqrt(variance + EPS) * gain + shift


def wide(ref, first, count):
    return jnp.concatenate([ref[tile, pl.ds(first, count), :] for tile in range(TILES)], 1)


def put_wide(ref, first, count, values):
    for tile in range(TILES):
        ref[tile, pl.ds(first, count), :] = values[:, 128 * tile : 128 * (tile + 1)]


def make_bias(rel_index, rel_table, table, bias):
    table[...] = jnp.zeros_like(table)
    table[:, pl.ds(0, rel_table.shape[1])] = rel_table[...]

    def rows_at(step, _):
        at = pl.multiple_of(step * 8, 8)
        for first, count in ((0, 128), (128, 16)):
            index = rel_index[pl.ds(at, 8), pl.ds(first, count)]
            if count < 128:
                index = jnp.concatenate([index, jnp.zeros((8, 128 - count), jnp.int32)], 1)
            low, high = index & 127, index >> 7
            for head in range(8):
                found = jnp.zeros((8, 128), F32)
                for part in range(6):
                    row = table[pl.ds(head, 1), pl.ds(128 * part, 128)]
                    drawn = jnp.take_along_axis(
                        jnp.broadcast_to(row, (8, 128)), low, axis=1, mode="promise_in_bounds"
                    )
                    found = jnp.where(high == part, drawn, found)
                bias[head, pl.ds(at, 8), pl.ds(first, count)] = found[:, :count]
        return 0

    lax.fori_loop(0, WTOK // 8, rows_at, 0)


def attend(qkv, attended, bias, marks, first):
    lane = lax.broadcasted_iota(jnp.int32, (1, 128), 1)
    left = lane < 64
    mark = marks[pl.ds(first, WTOK), :]
    barred = jnp.where(mark > 0, jnp.zeros_like(mark), jnp.full_like(mark, -1e30))
    ones = jnp.ones((WTOK, 128), BF16)
    for pair in range(4):
        query = qkv[pl.ds(first, WTOK), pl.ds(128 * pair, 128)]
        key = qkv[pl.ds(first, WTOK), pl.ds(512 + 128 * pair, 128)]
        value = qkv[pl.ds(first, WTOK), pl.ds(1024 + 128 * pair, 128)]
        keys = jnp.concatenate([key, barred], 1)
        values = jnp.concatenate([value, ones], 1)
        zero = jnp.zeros_like(query)
        results = []
        for side in range(2):
            part = jnp.where(left, query, zero) if side == 0 else jnp.where(left, zero, query)
            scores = lax.dot_general(
                jnp.concatenate([part, mark], 1), keys, (((1,), (1,)), ((), ())), preferred_element_type=F32
            )
            scores = scores + bias[2 * pair + side]
            powers = jnp.exp(scores - jnp.max(scores, -1, keepdims=True)).astype(BF16)
            total = jnp.dot(powers, values, preferred_element_type=F32)
            results.append(total[:, :128] / total[:, 128:])
        attended[pl.ds(first, WTOK), pl.ds(128 * pair, 128)] = jnp.where(left, results[0], results[1]).astype(BF16)


def spread(spots):
    token = lax.broadcasted_iota(jnp.int32, (WTOK, 128), 0)
    lev, row, col = token // 72, token // 12 % 6, token % 12
    spots[0] = lev * SIDE + row
    spots[1] = row
    spots[2] = col


def kinds(pair, regions, lat, lat_count):
    line = lax.broadcasted_iota(jnp.int32, (2 * SIDE, 128), 0)
    lev = jnp.where(line >= SIDE, 1, 0)
    row = line - SIDE * lev
    if pair == 0:
        row = jnp.where(row >= SIDE - 3, row - SIDE, row)
    else:
        row = jnp.where(row < 3, row + SIDE, row)
    whole = lat_count * SIDE
    orig = lat * SIDE + row
    orig = jnp.where(orig < 0, orig + whole, jnp.where(orig >= whole, orig - whole, orig))
    band = jnp.where(orig >= whole - 3, 1, 0)
    if pair == 1:
        band = band + 2 * lev
    return regions + (3 * band + 1).astype(F32)


def mark_window(ids, spots, marks, window, first):
    pair, wrow, wcol = window
    row0, col0 = CORNER[pair][0] + 6 * wrow, CORNER[pair][1] + 12 * wcol
    line, row, col = spots[0] + row0, spots[1], spots[2] + col0
    if row0 < 0:
        line = jnp.where(row < -row0, line + SIDE, line)
    elif row0 + 6 > SIDE:
        line = jnp.where(row >= SIDE - row0, line - SIDE, line)
    if col0 < 0:
        col = jnp.where(col < 0, col + SIDE, col)
    elif col0 + 12 > SIDE:
        col = jnp.where(col >= SIDE, col - SIDE, col)
    lane = lax.broadcasted_iota(jnp.int32, (WTOK, 128), 1)
    pick = jnp.where(lane == line, 1.0, 0.0).astype(BF16)
    rows = jnp.dot(pick, ids[pair].astype(BF16), preferred_element_type=F32)
    own = jnp.where(lane == col, rows, 0.0).astype(BF16)
    kind = jnp.dot(own, jnp.ones((128, 128), BF16), preferred_element_type=F32)
    marks[pl.ds(first, WTOK), :] = jnp.where(lane.astype(F32) + 1.0 == kind, 1.0, 0.0).astype(BF16)


def kernel(
    lat_count,
    lon_count,
    tokens,
    qkv_weight,
    proj_weight,
    fc1_weight,
    fc2_weight,
    merge_weight,
    region,
    rel_index,
    rel_table,
    norm1_gain,
    norm1_bias,
    qkv_bias,
    proj_bias,
    norm2_gain,
    norm2_bias,
    fc1_bias,
    fc2_bias,
    merge_gain,
    merge_bias,
    out,
    block,
    part,
    wq,
    wp,
    w1,
    w2,
    wm,
    bias,
    marks,
    normed,
    qkv,
    attended,
    active,
    normed3,
    product,
    table,
    own_ids,
    far_ids,
    ids,
    spots,
    halo_out,
    halo_in,
    back_out,
    back_in,
    load_sem,
    id_send,
    id_recv,
    halo_send,
    halo_recv,
    back_send,
    back_recv,
):
    lat, lon = lax.axis_index("lat"), lax.axis_index("lon")

    def device(rows, cols):
        return lax.rem(lat + rows + lat_count, lat_count), lax.rem(lon + cols + lon_count, lon_count)

    barrier = pltpu.get_barrier_semaphore()
    around = ((0, 1), (1, 0), (1, 1), (0, -1), (-1, 0), (-1, -1))
    for away in around:
        pl.semaphore_signal(barrier, inc=1, device_id=device(*away), device_id_type=MESH)

    def token_load(tile):
        return pltpu.make_async_copy(
            tokens.at[:, pl.ds(128 * tile, 128)], block.at[tile, pl.ds(0, TOKENS)], load_sem.at[tile]
        )

    for tile in range(TILES):
        token_load(tile).start()

    loads = [
        pltpu.make_async_copy(source, target, load_sem.at[TILES + number])
        for number, (source, target) in enumerate(
            ((qkv_weight, wq), (proj_weight, wp), (fc1_weight, w1), (fc2_weight, w2), (merge_weight, wm))
        )
    ]

    own_ids[...] = jnp.zeros_like(own_ids)
    for pair in range(2):
        for lev in range(2):
            own_ids[pair, pl.ds(SIDE * lev, SIDE), pl.ds(0, SIDE)] = region[LEVELS[pair][lev]].astype(F32)
    block[:, pl.ds(TOKENS, 16), :] = jnp.zeros((TILES, 16, 128), F32)
    for pair in range(2):
        for slot in (3, 5, 6):
            halo_out[pair, slot, :, pl.ds(32, 8), :] = jnp.zeros((TILES, 8, 128), F32)
            back_out[pair, slot, :, pl.ds(32, 8), :] = jnp.zeros((TILES, 8, 128), F32)

    def id_copy(pair, side):
        rows, cols = ((0, 1), (1, 0), (1, 1))[side]
        sign = 1 if pair == 0 else -1
        return pltpu.make_async_remote_copy(
            src_ref=own_ids.at[pair],
            dst_ref=far_ids.at[pair, side],
            send_sem=id_send.at[pair, side],
            recv_sem=id_recv.at[pair, side],
            device_id=device(sign * rows, sign * cols),
            device_id_type=MESH,
        )

    def piece_copy(pair, slot, back):
        rows, cols = FROM[slot]
        sign = (1 if pair == 0 else -1) * (1 if back else -1)
        size = SLOT if slot in (0, 1, 2, 4) else 40
        source, target = (back_out, back_in) if back else (halo_out, halo_in)
        send, recv = (back_send, back_recv) if back else (halo_send, halo_recv)
        return pltpu.make_async_remote_copy(
            src_ref=source.at[pair, slot, :, pl.ds(0, size)],
            dst_ref=target.at[pair, slot, :, pl.ds(0, size)],
            send_sem=send.at[pair, slot],
            recv_sem=recv.at[pair, slot],
            device_id=device(sign * rows, sign * cols),
            device_id_type=MESH,
        )

    order = [slot for step in STEPS for slot in slots_of(step)]
    late = slots_of(STEPS[LOOPED[2]])

    for tile in range(TILES):
        token_load(tile).wait()
    for load in loads:
        load.start()
    for pair, slot in order:
        for first, count, where in piece_runs(pair, slot):
            halo_out[pair, slot, :, pl.ds(first, count), :] = block[:, pl.ds(where, count), :]
    pl.semaphore_wait(barrier, len(around))
    for pair in range(2):
        for side in range(3):
            id_copy(pair, side).start()
    for pair, slot in order:
        if (pair, slot) not in late:
            piece_copy(pair, slot, False).start()

    ids[...] = jnp.zeros_like(ids)
    for pair in range(2):
        ids[pair, pl.ds(0, 2 * SIDE), :] = kinds(pair, own_ids[pair], lat, lat_count)
    spread(spots)
    make_bias(rel_index, rel_table, table, bias)

    def all_ids():
        for pair in range(2):
            for side in range(3):
                id_copy(pair, side).wait()
            line = lax.broadcasted_iota(jnp.int32, (2 * SIDE, 128), 0)
            line = jnp.where(line >= SIDE, line - SIDE, line)
            lane = lax.broadcasted_iota(jnp.int32, (2 * SIDE, 128), 1)
            far_row = line >= SIDE - 3 if pair == 0 else line < 3
            far_col = lane >= SIDE - 6 if pair == 0 else lane < 6
            regions = jnp.where(
                far_row,
                jnp.where(far_col, far_ids[pair, 2], far_ids[pair, 1]),
                jnp.where(far_col, far_ids[pair, 0], own_ids[pair]),
            )
            ids[pair, pl.ds(0, 2 * SIDE), :] = kinds(pair, regions, lat, lat_count)

    for load in loads[:-1]:
        load.wait()

    def first_norm(first, count):
        for place in range(first, first + count):
            normed[pl.ds(place * WTOK, WTOK), :] = norm(
                wide(part, place * WTOK, WTOK), norm1_gain[...], norm1_bias[...]
            ).astype(BF16)

    def pack(first, count):
        at = pl.ds(first * WTOK, count * WTOK)
        for third in range(3):
            columns = pl.ds(512 * third, 512)
            packed = jnp.dot(normed[at, :], wq[:, columns], preferred_element_type=F32)
            packed = packed + qkv_bias[columns].reshape(1, 512)
            if third == 0:
                packed = packed * 0.125
            qkv[at, columns] = packed.astype(BF16)

    def project(first, count):
        first, count = first * WTOK, count * WTOK
        at = pl.ds(first, count)
        hidden = jnp.dot(attended[at, :], wp[...], preferred_element_type=F32) + proj_bias[...]
        hidden = hidden + wide(part, first, count)
        put_wide(part, first, count, hidden)
        normed[at, :] = norm(hidden, norm2_gain[...], norm2_bias[...]).astype(BF16)

    def expand(first, count, quarter):
        at = pl.ds(first * WTOK, count * WTOK)
        columns = pl.ds(512 * quarter, 512)
        units = jnp.dot(normed[at, :], w1[:, columns], preferred_element_type=F32) + fc1_bias[:, columns]
        active[at, columns] = (0.5 * units * (1.0 + lax.erf(units * 0.7071067811865476))).astype(BF16)

    def contract(first, count):
        first, count = first * WTOK, count * WTOK
        result = jnp.dot(active[pl.ds(first, count), :], w2[...], preferred_element_type=F32) + fc2_bias[...]
        put_wide(part, first, count, result + wide(part, first, count))

    def compute(count):
        first_norm(0, count)
        pack(0, count)
        half = count // 2 if count > 2 else count
        early = half + half // 2 if count > 2 else count
        for place in range(early):
            attend(qkv, attended, bias, marks, place * WTOK)
        project(0, half)
        for place in range(early, count):
            attend(qkv, attended, bias, marks, place * WTOK)
        for quarter in range(4):
            expand(0, half, quarter)
        if half < count:
            project(half, half)
        contract(0, half)
        if half < count:
            for quarter in range(4):
                expand(half, half, quarter)
            contract(half, half)

    def gather(number):
        windows = STEPS[number]
        if number == 1:
            for pair, slot in late:
                piece_copy(pair, slot, False).start()
            all_ids()
        for pair, slot in slots_of(windows):
            piece_copy(pair, slot, False).wait_recv()
        for place, window in enumerate(windows):
            for token, count, slot, first in segments(window):
                at = pl.ds(place * WTOK + token, count)
                if slot is None:
                    part[:, at, :] = block[:, pl.ds(first, count), :]
                else:
                    part[:, at, :] = halo_in[window[0], slot, :, pl.ds(first, count), :]
            mark_window(ids, spots, marks, window, place * WTOK)

    def settle(number):
        windows = STEPS[number]
        for place, window in enumerate(windows):
            for token, count, slot, first in segments(window):
                at = pl.ds(place * WTOK + token, count)
                if slot is not None:
                    back_out[window[0], slot, :, pl.ds(first, count), :] = part[:, at, :]
        for pair, slot in slots_of(windows):
            piece_copy(pair, slot, True).start()
        for place, window in enumerate(windows):
            for token, count, slot, first in segments(window):
                at = pl.ds(place * WTOK + token, count)
                if slot is None:
                    block[:, pl.ds(first, count), :] = part[:, at, :]

    def short(number):
        gather(number)
        compute(len(STEPS[number]))
        settle(number)

    def run(step, _):
        for at, number in enumerate(LOOPED):
            if at == 2:
                pl.when(step == at)(functools.partial(short, BETWEEN))
            pl.when(step == at)(functools.partial(gather, number))
        compute(G)
        for at, number in enumerate(LOOPED):
            pl.when(step == at)(functools.partial(settle, number))
        return 0

    lax.fori_loop(0, len(LOOPED), run, 0)
    short(LAST)

    def merge(part_of, rows):
        for pair, slot in order:
            if (slot > 2) == (part_of == 1):
                piece_copy(pair, slot, True).wait_recv()
                for first, count, where in piece_runs(pair, slot):
                    block[:, pl.ds(where, count), :] = back_in[pair, slot, :, pl.ds(first, count), :]
        if part_of == 0:
            loads[-1].wait()
        levels = 8 // len(rows)

        def merge_norm(step, _):
            for number in range(8):
                at = step * 8 + number
                line = (step * levels + number // len(rows)) * 12 + rows[number % len(rows)]
                values = jnp.concatenate(
                    [
                        block[tile, pl.ds(line * 2 * SIDE + row * SIDE + col, 16, stride=2), :]
                        for col in range(2)
                        for row in range(2)
                        for tile in range(TILES)
                    ],
                    1,
                )
                normed3[pl.ds(pl.multiple_of(at * 16, 16), 16), :] = norm(
                    values, merge_gain[...], merge_bias[...]
                ).astype(BF16)
            return 0

        lax.fori_loop(0, 4 // levels, merge_norm, 0)
        for quarter in range(4):
            merged = jnp.dot(
                normed3[pl.ds(0, 64 * len(rows)), :],
                wm[:, pl.ds(256 * quarter, 256)],
                preferred_element_type=F32,
            )
            for at in range(4 * len(rows)):
                first = rows[at % len(rows)] * 48 + at // len(rows)
                for half in range(2):
                    product[2 * quarter + half, pl.ds(first, 12, stride=4), :] = merged[
                        16 * at : 16 * at + 12, 128 * half : 128 * (half + 1)
                    ]

    for part_of, rows in enumerate(LINES):
        merge(part_of, rows)
    for tile in range(8):
        out[:, :, pl.ds(128 * tile, 128)] = product[tile].astype(BF16).reshape(144, 4, 128)

    for pair, slot in order:
        piece_copy(pair, slot, False).wait_send()
        piece_copy(pair, slot, True).wait_send()


def per_device(mesh_shape, tokens, region, rel_index, rel_table, *rest):
    (
        norm1_gain,
        norm1_bias,
        qkv_weight,
        qkv_bias,
        proj_weight,
        proj_bias,
        norm2_gain,
        norm2_bias,
        fc1_weight,
        fc1_bias,
        fc2_weight,
        fc2_bias,
        merge_gain,
        merge_bias,
        merge_weight,
    ) = rest
    lines = [
        value.reshape(1, -1)
        for value in (
            norm1_gain,
            norm1_bias,
            proj_bias,
            norm2_gain,
            norm2_bias,
            fc1_bias,
            fc2_bias,
            merge_gain,
            merge_bias,
        )
    ]
    lines.insert(2, qkv_bias)
    hbm = pl.BlockSpec(memory_space=pl.ANY)
    vmem = pl.BlockSpec(memory_space=pltpu.VMEM)
    merged = pl.pallas_call(
        functools.partial(kernel, *mesh_shape),
        out_shape=pltpu.VMEM((144, 4, 1024), BF16),
        in_specs=[hbm] * 6 + [vmem] * 13,
        out_specs=vmem,
        scratch_shapes=[
            pltpu.VMEM((TILES, TOKENS + 16, 128), F32),
            pltpu.VMEM((TILES, ROWS, 128), F32),
            pltpu.VMEM((512, 1536), BF16),
            pltpu.VMEM((512, 512), BF16),
            pltpu.VMEM((512, 2048), BF16),
            pltpu.VMEM((2048, 512), BF16),
            pltpu.VMEM((2048, 1024), BF16),
            pltpu.VMEM((8, WTOK, WTOK), F32),
            pltpu.VMEM((ROWS, 128), BF16),
            pltpu.VMEM((ROWS, 512), BF16),
            pltpu.VMEM((ROWS, 1536), BF16),
            pltpu.VMEM((ROWS, 512), BF16),
            pltpu.VMEM((ROWS, 2048), BF16),
            pltpu.VMEM((512, 2048), BF16),
            pltpu.VMEM((8, 576, 128), F32),
            pltpu.VMEM((8, 768), F32),
            pltpu.VMEM((2, 2 * SIDE, 128), F32),
            pltpu.VMEM((2, 3, 2 * SIDE, 128), F32),
            pltpu.VMEM((2, 128, 128), F32),
            pltpu.VMEM((3, WTOK, 128), jnp.int32),
        ]
        + [pltpu.VMEM((2, 7, TILES, SLOT, 128), F32)] * 4
        + [
            pltpu.SemaphoreType.DMA((TILES + 5,)),
            pltpu.SemaphoreType.DMA((2, 3)),
            pltpu.SemaphoreType.DMA((2, 3)),
        ]
        + [pltpu.SemaphoreType.DMA((2, 7))] * 4,
        compiler_params=pltpu.CompilerParams(
            collective_id=0, has_side_effects=True, vmem_limit_bytes=60 * 2**20
        ),
        name="block",
    )(
        tokens.reshape(TOKENS, 512),
        qkv_weight,
        proj_weight,
        fc1_weight,
        fc2_weight,
        merge_weight,
        region,
        rel_index,
        rel_table,
        *lines,
    )
    return merged.reshape(12, 12, 4, 1024).transpose(2, 0, 1, 3)


def solution(mesh):
    shape = (mesh.shape["lat"], mesh.shape["lon"])
    return jax.shard_map(
        functools.partial(per_device, shape),
        mesh=mesh,
        in_specs=(P(None, "lat", "lon", None), P(None, "lat", "lon")) + (P(),) * 17,
        out_specs=P(None, "lat", "lon", None),
        check_vma=False,
    )
```

```python
import functools

import jax
import jax.numpy as jnp
from jax import lax
from jax.experimental import pallas as pl
from jax.experimental.pallas import tpu as pltpu
from jax.sharding import PartitionSpec as P

MESH = pl.DeviceIdType.MESH
F32 = jnp.float32
BF16 = jnp.bfloat16
EPS = 1e-05
SIDE = 24
WTOK = 144
G = 4
ROWS = G * WTOK
TOKENS = 4 * SIDE * SIDE
TILES = 4
SLOT = 72

LEVELS = ((1, 2), (3, 0))
CORNER = ((-3, -6), (3, 6))
PIECES = (
    ((3, 6, 18, 6), (9, 6, 18, 6), (15, 6, 18, 6), (0, 3, 18, 6), (21, 3, 6, 12), (21, 3, 0, 6), (21, 3, 18, 6)),
    ((3, 6, 0, 6), (9, 6, 0, 6), (15, 6, 0, 6), (21, 3, 0, 6), (0, 3, 6, 12), (0, 3, 18, 6), (0, 3, 0, 6)),
)
FROM = ((0, -1), (0, -1), (0, -1), (0, -1), (-1, 0), (-1, 0), (-1, -1))
STEPS = (
    ((0, 1, 1), (0, 2, 1), (1, 0, 0), (1, 1, 0)),
    ((0, 1, 0), (0, 2, 0), (0, 3, 0), (1, 0, 1)),
    ((1, 1, 1), (1, 2, 1)),
    ((0, 0, 0), (0, 0, 1), (1, 3, 1), (1, 3, 0)),
    ((0, 3, 1), (1, 2, 0)),
)
LOOPED = (0, 1, 3)
BETWEEN, LAST = 2, 4
LINES = (tuple(range(2, 10)), (0, 1, 10, 11))


def segments(window):
    pair, wrow, wcol = window
    row0, col0 = CORNER[pair][0] + 6 * wrow, CORNER[pair][1] + 12 * wcol
    runs = []
    for lev in range(2):
        for row in range(6):
            for half in range(2):
                at_row, at_col = row0 + row, col0 + 6 * half
                where_row, where_col = at_row % SIDE, at_col % SIDE
                away = (at_row // SIDE, at_col // SIDE)
                token = (lev * 6 + row) * 12 + 6 * half
                if away == (0, 0):
                    slot, first = None, (LEVELS[pair][lev] * SIDE + where_row) * SIDE + where_col
                else:
                    slot = None
                    for number, (first_row, rows, first_col, cols) in enumerate(PIECES[pair]):
                        if first_row <= where_row < first_row + rows and first_col <= where_col < first_col + cols:
                            slot = number
                            first = (lev * rows + where_row - first_row) * cols + where_col - first_col
                if runs and runs[-1][2] == slot and runs[-1][0] + runs[-1][1] == token and runs[-1][3] + runs[-1][1] == first:
                    runs[-1] = (runs[-1][0], runs[-1][1] + 6, slot, runs[-1][3])
                else:
                    runs.append((token, 6, slot, first))
    return runs


def slots_of(windows):
    return [
        (window[0], slot)
        for window in windows
        for slot in sorted({run[2] for run in segments(window) if run[2] is not None})
    ]


def piece_runs(pair, slot):
    first_row, rows, first_col, cols = PIECES[pair][slot]
    for lev in range(2):
        for row in range(rows):
            yield (lev * rows + row) * cols, cols, (LEVELS[pair][lev] * SIDE + first_row + row) * SIDE + first_col


def norm(values, gain, shift):
    centred = values - jnp.mean(values, -1, keepdims=True)
    variance = jnp.mean(centred * centred, -1, keepdims=True)
    return centred * lax.rsqrt(variance + EPS) * gain + shift


def wide(ref, first, count):
    return jnp.concatenate([ref[tile, pl.ds(first, count), :] for tile in range(TILES)], 1)


def put_wide(ref, first, count, values):
    for tile in range(TILES):
        ref[tile, pl.ds(first, count), :] = values[:, 128 * tile : 128 * (tile + 1)]


def make_bias(rel_index, rel_table, table, bias):
    table[...] = jnp.zeros_like(table)
    table[:, pl.ds(0, rel_table.shape[1])] = rel_table[...]

    def rows_at(step, _):
        at = pl.multiple_of(step * 8, 8)
        for first, count in ((0, 128), (128, 16)):
            index = rel_index[pl.ds(at, 8), pl.ds(first, count)]
            if count < 128:
                index = jnp.concatenate([index, jnp.zeros((8, 128 - count), jnp.int32)], 1)
            low, high = index & 127, index >> 7
            for head in range(8):
                found = jnp.zeros((8, 128), F32)
                for part in range(6):
                    row = table[pl.ds(head, 1), pl.ds(128 * part, 128)]
                    drawn = jnp.take_along_axis(
                        jnp.broadcast_to(row, (8, 128)), low, axis=1, mode="promise_in_bounds"
                    )
                    found = jnp.where(high == part, drawn, found)
                bias[head, pl.ds(at, 8), pl.ds(first, count)] = found[:, :count]
        return 0

    lax.fori_loop(0, WTOK // 8, rows_at, 0)


def attend(qkv, attended, bias, marks, first):
    lane = lax.broadcasted_iota(jnp.int32, (1, 128), 1)
    left = lane < 64
    mark = marks[pl.ds(first, WTOK), :]
    barred = jnp.where(mark > 0, jnp.zeros_like(mark), jnp.full_like(mark, -1e30))
    ones = jnp.ones((WTOK, 128), BF16)
    for pair in range(4):
        query = qkv[pl.ds(first, WTOK), pl.ds(128 * pair, 128)]
        key = qkv[pl.ds(first, WTOK), pl.ds(512 + 128 * pair, 128)]
        value = qkv[pl.ds(first, WTOK), pl.ds(1024 + 128 * pair, 128)]
        keys = jnp.concatenate([key, barred], 1)
        values = jnp.concatenate([value, ones], 1)
        zero = jnp.zeros_like(query)
        results = []
        for side in range(2):
            part = jnp.where(left, query, zero) if side == 0 else jnp.where(left, zero, query)
            scores = lax.dot_general(
                jnp.concatenate([part, mark], 1), keys, (((1,), (1,)), ((), ())), preferred_element_type=F32
            )
            scores = scores + bias[2 * pair + side]
            powers = jnp.exp(scores - jnp.max(scores, -1, keepdims=True)).astype(BF16)
            total = jnp.dot(powers, values, preferred_element_type=F32)
            results.append(total[:, :128] / total[:, 128:])
        attended[pl.ds(first, WTOK), pl.ds(128 * pair, 128)] = jnp.where(left, results[0], results[1]).astype(BF16)


def spread(spots):
    token = lax.broadcasted_iota(jnp.int32, (WTOK, 128), 0)
    lev, row, col = token // 72, token // 12 % 6, token % 12
    spots[0] = lev * SIDE + row
    spots[1] = row
    spots[2] = col


def kinds(pair, regions, lat, lat_count):
    line = lax.broadcasted_iota(jnp.int32, (2 * SIDE, 128), 0)
    lev = jnp.where(line >= SIDE, 1, 0)
    row = line - SIDE * lev
    if pair == 0:
        row = jnp.where(row >= SIDE - 3, row - SIDE, row)
    else:
        row = jnp.where(row < 3, row + SIDE, row)
    whole = lat_count * SIDE
    orig = lat * SIDE + row
    orig = jnp.where(orig < 0, orig + whole, jnp.where(orig >= whole, orig - whole, orig))
    band = jnp.where(orig >= whole - 3, 1, 0)
    if pair == 1:
        band = band + 2 * lev
    return regions + (3 * band + 1).astype(F32)


def mark_window(ids, spots, marks, window, first):
    pair, wrow, wcol = window
    row0, col0 = CORNER[pair][0] + 6 * wrow, CORNER[pair][1] + 12 * wcol
    line, row, col = spots[0] + row0, spots[1], spots[2] + col0
    if row0 < 0:
        line = jnp.where(row < -row0, line + SIDE, line)
    elif row0 + 6 > SIDE:
        line = jnp.where(row >= SIDE - row0, line - SIDE, line)
    if col0 < 0:
        col = jnp.where(col < 0, col + SIDE, col)
    elif col0 + 12 > SIDE:
        col = jnp.where(col >= SIDE, col - SIDE, col)
    lane = lax.broadcasted_iota(jnp.int32, (WTOK, 128), 1)
    pick = jnp.where(lane == line, 1.0, 0.0).astype(BF16)
    rows = jnp.dot(pick, ids[pair].astype(BF16), preferred_element_type=F32)
    own = jnp.where(lane == col, rows, 0.0).astype(BF16)
    kind = jnp.dot(own, jnp.ones((128, 128), BF16), preferred_element_type=F32)
    marks[pl.ds(first, WTOK), :] = jnp.where(lane.astype(F32) + 1.0 == kind, 1.0, 0.0).astype(BF16)


def kernel(
    lat_count,
    lon_count,
    tokens,
    qkv_weight,
    proj_weight,
    fc1_weight,
    fc2_weight,
    merge_weight,
    region,
    rel_index,
    rel_table,
    norm1_gain,
    norm1_bias,
    qkv_bias,
    proj_bias,
    norm2_gain,
    norm2_bias,
    fc1_bias,
    fc2_bias,
    merge_gain,
    merge_bias,
    out,
    block,
    part,
    wq,
    wp,
    w1,
    w2,
    wm,
    bias,
    marks,
    normed,
    qkv,
    attended,
    active,
    normed3,
    product,
    table,
    own_ids,
    far_ids,
    ids,
    spots,
    halo_out,
    halo_in,
    back_out,
    back_in,
    load_sem,
    id_send,
    id_recv,
    halo_send,
    halo_recv,
    back_send,
    back_recv,
):
    lat, lon = lax.axis_index("lat"), lax.axis_index("lon")

    def device(rows, cols):
        return lax.rem(lat + rows + lat_count, lat_count), lax.rem(lon + cols + lon_count, lon_count)

    barrier = pltpu.get_barrier_semaphore()
    around = ((0, 1), (1, 0), (1, 1), (0, -1), (-1, 0), (-1, -1))
    for away in around:
        pl.semaphore_signal(barrier, inc=1, device_id=device(*away), device_id_type=MESH)

    def token_load(tile):
        return pltpu.make_async_copy(
            tokens.at[:, pl.ds(128 * tile, 128)], block.at[tile, pl.ds(0, TOKENS)], load_sem.at[tile]
        )

    for tile in range(TILES):
        token_load(tile).start()

    loads = [
        pltpu.make_async_copy(source, target, load_sem.at[TILES + number])
        for number, (source, target) in enumerate(
            ((qkv_weight, wq), (proj_weight, wp), (fc1_weight, w1), (fc2_weight, w2), (merge_weight, wm))
        )
    ]

    own_ids[...] = jnp.zeros_like(own_ids)
    for pair in range(2):
        for lev in range(2):
            own_ids[pair, pl.ds(SIDE * lev, SIDE), pl.ds(0, SIDE)] = region[LEVELS[pair][lev]].astype(F32)
    block[:, pl.ds(TOKENS, 16), :] = jnp.zeros((TILES, 16, 128), F32)
    for pair in range(2):
        for slot in (3, 5, 6):
            halo_out[pair, slot, :, pl.ds(32, 8), :] = jnp.zeros((TILES, 8, 128), F32)
            back_out[pair, slot, :, pl.ds(32, 8), :] = jnp.zeros((TILES, 8, 128), F32)

    def id_copy(pair, side):
        rows, cols = ((0, 1), (1, 0), (1, 1))[side]
        sign = 1 if pair == 0 else -1
        return pltpu.make_async_remote_copy(
            src_ref=own_ids.at[pair],
            dst_ref=far_ids.at[pair, side],
            send_sem=id_send.at[pair, side],
            recv_sem=id_recv.at[pair, side],
            device_id=device(sign * rows, sign * cols),
            device_id_type=MESH,
        )

    def piece_copy(pair, slot, back):
        rows, cols = FROM[slot]
        sign = (1 if pair == 0 else -1) * (1 if back else -1)
        size = SLOT if slot in (0, 1, 2, 4) else 40
        source, target = (back_out, back_in) if back else (halo_out, halo_in)
        send, recv = (back_send, back_recv) if back else (halo_send, halo_recv)
        return pltpu.make_async_remote_copy(
            src_ref=source.at[pair, slot, :, pl.ds(0, size)],
            dst_ref=target.at[pair, slot, :, pl.ds(0, size)],
            send_sem=send.at[pair, slot],
            recv_sem=recv.at[pair, slot],
            device_id=device(sign * rows, sign * cols),
            device_id_type=MESH,
        )

    order = [slot for step in STEPS for slot in slots_of(step)]
    late = slots_of(STEPS[LOOPED[2]])

    for tile in range(TILES):
        token_load(tile).wait()
    for load in loads:
        load.start()
    def fill(pieces):
        for pair, slot in pieces:
            for first, count, where in piece_runs(pair, slot):
                halo_out[pair, slot, :, pl.ds(first, count), :] = block[:, pl.ds(where, count), :]

    soon = [piece for piece in order if piece not in late]
    fill(soon)
    pl.semaphore_wait(barrier, len(around))
    for pair, slot in soon:
        piece_copy(pair, slot, False).start()
    for pair in range(2):
        for side in range(3):
            id_copy(pair, side).start()
    fill(late)

    ids[...] = jnp.zeros_like(ids)
    for pair in range(2):
        ids[pair, pl.ds(0, 2 * SIDE), :] = kinds(pair, own_ids[pair], lat, lat_count)
    spread(spots)
    make_bias(rel_index, rel_table, table, bias)

    def all_ids():
        for pair in range(2):
            for side in range(3):
                id_copy(pair, side).wait()
            line = lax.broadcasted_iota(jnp.int32, (2 * SIDE, 128), 0)
            line = jnp.where(line >= SIDE, line - SIDE, line)
            lane = lax.broadcasted_iota(jnp.int32, (2 * SIDE, 128), 1)
            far_row = line >= SIDE - 3 if pair == 0 else line < 3
            far_col = lane >= SIDE - 6 if pair == 0 else lane < 6
            regions = jnp.where(
                far_row,
                jnp.where(far_col, far_ids[pair, 2], far_ids[pair, 1]),
                jnp.where(far_col, far_ids[pair, 0], own_ids[pair]),
            )
            ids[pair, pl.ds(0, 2 * SIDE), :] = kinds(pair, regions, lat, lat_count)

    for load in loads[:-1]:
        load.wait()

    def first_norm(first, count):
        for place in range(first, first + count):
            normed[pl.ds(place * WTOK, WTOK), :] = norm(
                wide(part, place * WTOK, WTOK), norm1_gain[...], norm1_bias[...]
            ).astype(BF16)

    def pack(first, count):
        at = pl.ds(first * WTOK, count * WTOK)
        for third in range(3):
            columns = pl.ds(512 * third, 512)
            packed = jnp.dot(normed[at, :], wq[:, columns], preferred_element_type=F32)
            packed = packed + qkv_bias[columns].reshape(1, 512)
            if third == 0:
                packed = packed * 0.125
            qkv[at, columns] = packed.astype(BF16)

    def project(first, count):
        first, count = first * WTOK, count * WTOK
        at = pl.ds(first, count)
        hidden = jnp.dot(attended[at, :], wp[...], preferred_element_type=F32) + proj_bias[...]
        hidden = hidden + wide(part, first, count)
        put_wide(part, first, count, hidden)
        normed[at, :] = norm(hidden, norm2_gain[...], norm2_bias[...]).astype(BF16)

    def expand(first, count, quarter):
        at = pl.ds(first * WTOK, count * WTOK)
        columns = pl.ds(512 * quarter, 512)
        units = jnp.dot(normed[at, :], w1[:, columns], preferred_element_type=F32) + fc1_bias[:, columns]
        active[at, columns] = (0.5 * units * (1.0 + lax.erf(units * 0.7071067811865476))).astype(BF16)

    def contract(first, count):
        first, count = first * WTOK, count * WTOK
        result = jnp.dot(active[pl.ds(first, count), :], w2[...], preferred_element_type=F32) + fc2_bias[...]
        put_wide(part, first, count, result + wide(part, first, count))

    def compute(count):
        first_norm(0, count)
        pack(0, count)
        half = count // 2 if count > 2 else count
        early = half + half // 2 if count > 2 else count
        for place in range(early):
            attend(qkv, attended, bias, marks, place * WTOK)
        project(0, half)
        for place in range(early, count):
            attend(qkv, attended, bias, marks, place * WTOK)
        for quarter in range(4):
            expand(0, half, quarter)
        if half < count:
            project(half, half)
        contract(0, half)
        if half < count:
            for quarter in range(4):
                expand(half, half, quarter)
            contract(half, half)

    def gather(number):
        windows = STEPS[number]
        if number == 1:
            for pair, slot in late:
                piece_copy(pair, slot, False).start()
            all_ids()
        for pair, slot in slots_of(windows):
            piece_copy(pair, slot, False).wait_recv()
        for place, window in enumerate(windows):
            for token, count, slot, first in segments(window):
                at = pl.ds(place * WTOK + token, count)
                if slot is None:
                    part[:, at, :] = block[:, pl.ds(first, count), :]
                else:
                    part[:, at, :] = halo_in[window[0], slot, :, pl.ds(first, count), :]
            mark_window(ids, spots, marks, window, place * WTOK)

    def settle(number):
        windows = STEPS[number]
        for place, window in enumerate(windows):
            for token, count, slot, first in segments(window):
                at = pl.ds(place * WTOK + token, count)
                if slot is not None:
                    back_out[window[0], slot, :, pl.ds(first, count), :] = part[:, at, :]
        for pair, slot in slots_of(windows):
            piece_copy(pair, slot, True).start()
        for place, window in enumerate(windows):
            for token, count, slot, first in segments(window):
                at = pl.ds(place * WTOK + token, count)
                if slot is None:
                    block[:, pl.ds(first, count), :] = part[:, at, :]

    def short(number):
        gather(number)
        compute(len(STEPS[number]))
        settle(number)

    def run(step, _):
        for at, number in enumerate(LOOPED):
            if at == 2:
                pl.when(step == at)(functools.partial(short, BETWEEN))
            pl.when(step == at)(functools.partial(gather, number))
        compute(G)
        for at, number in enumerate(LOOPED):
            pl.when(step == at)(functools.partial(settle, number))
        return 0

    lax.fori_loop(0, len(LOOPED), run, 0)
    short(LAST)

    def merge(part_of, rows):
        for pair, slot in order:
            if (slot > 2) == (part_of == 1):
                piece_copy(pair, slot, True).wait_recv()
                for first, count, where in piece_runs(pair, slot):
                    block[:, pl.ds(where, count), :] = back_in[pair, slot, :, pl.ds(first, count), :]
        if part_of == 0:
            loads[-1].wait()
        levels = 8 // len(rows)

        def merge_norm(step, _):
            for number in range(8):
                at = step * 8 + number
                line = (step * levels + number // len(rows)) * 12 + rows[number % len(rows)]
                values = jnp.concatenate(
                    [
                        block[tile, pl.ds(line * 2 * SIDE + row * SIDE + col, 16, stride=2), :]
                        for col in range(2)
                        for row in range(2)
                        for tile in range(TILES)
                    ],
                    1,
                )
                normed3[pl.ds(pl.multiple_of(at * 16, 16), 16), :] = norm(
                    values, merge_gain[...], merge_bias[...]
                ).astype(BF16)
            return 0

        lax.fori_loop(0, 4 // levels, merge_norm, 0)
        for quarter in range(4):
            merged = jnp.dot(
                normed3[pl.ds(0, 64 * len(rows)), :],
                wm[:, pl.ds(256 * quarter, 256)],
                preferred_element_type=F32,
            )
            for at in range(4 * len(rows)):
                first = rows[at % len(rows)] * 48 + at // len(rows)
                for half in range(2):
                    product[2 * quarter + half, pl.ds(first, 12, stride=4), :] = merged[
                        16 * at : 16 * at + 12, 128 * half : 128 * (half + 1)
                    ]

    for part_of, rows in enumerate(LINES):
        merge(part_of, rows)
    for tile in range(8):
        out[:, :, pl.ds(128 * tile, 128)] = product[tile].astype(BF16).reshape(144, 4, 128)

    for pair, slot in order:
        piece_copy(pair, slot, False).wait_send()
        piece_copy(pair, slot, True).wait_send()


def per_device(mesh_shape, tokens, region, rel_index, rel_table, *rest):
    (
        norm1_gain,
        norm1_bias,
        qkv_weight,
        qkv_bias,
        proj_weight,
        proj_bias,
        norm2_gain,
        norm2_bias,
        fc1_weight,
        fc1_bias,
        fc2_weight,
        fc2_bias,
        merge_gain,
        merge_bias,
        merge_weight,
    ) = rest
    lines = [
        value.reshape(1, -1)
        for value in (
            norm1_gain,
            norm1_bias,
            proj_bias,
            norm2_gain,
            norm2_bias,
            fc1_bias,
            fc2_bias,
            merge_gain,
            merge_bias,
        )
    ]
    lines.insert(2, qkv_bias)
    hbm = pl.BlockSpec(memory_space=pl.ANY)
    vmem = pl.BlockSpec(memory_space=pltpu.VMEM)
    merged = pl.pallas_call(
        functools.partial(kernel, *mesh_shape),
        out_shape=pltpu.VMEM((144, 4, 1024), BF16),
        in_specs=[hbm] * 6 + [vmem] * 13,
        out_specs=vmem,
        scratch_shapes=[
            pltpu.VMEM((TILES, TOKENS + 16, 128), F32),
            pltpu.VMEM((TILES, ROWS, 128), F32),
            pltpu.VMEM((512, 1536), BF16),
            pltpu.VMEM((512, 512), BF16),
            pltpu.VMEM((512, 2048), BF16),
            pltpu.VMEM((2048, 512), BF16),
            pltpu.VMEM((2048, 1024), BF16),
            pltpu.VMEM((8, WTOK, WTOK), F32),
            pltpu.VMEM((ROWS, 128), BF16),
            pltpu.VMEM((ROWS, 512), BF16),
            pltpu.VMEM((ROWS, 1536), BF16),
            pltpu.VMEM((ROWS, 512), BF16),
            pltpu.VMEM((ROWS, 2048), BF16),
            pltpu.VMEM((512, 2048), BF16),
            pltpu.VMEM((8, 576, 128), F32),
            pltpu.VMEM((8, 768), F32),
            pltpu.VMEM((2, 2 * SIDE, 128), F32),
            pltpu.VMEM((2, 3, 2 * SIDE, 128), F32),
            pltpu.VMEM((2, 128, 128), F32),
            pltpu.VMEM((3, WTOK, 128), jnp.int32),
        ]
        + [pltpu.VMEM((2, 7, TILES, SLOT, 128), F32)] * 4
        + [
            pltpu.SemaphoreType.DMA((TILES + 5,)),
            pltpu.SemaphoreType.DMA((2, 3)),
            pltpu.SemaphoreType.DMA((2, 3)),
        ]
        + [pltpu.SemaphoreType.DMA((2, 7))] * 4,
        compiler_params=pltpu.CompilerParams(
            collective_id=0, has_side_effects=True, vmem_limit_bytes=60 * 2**20
        ),
        name="block",
    )(
        tokens.reshape(TOKENS, 512),
        qkv_weight,
        proj_weight,
        fc1_weight,
        fc2_weight,
        merge_weight,
        region,
        rel_index,
        rel_table,
        *lines,
    )
    return merged.reshape(12, 12, 4, 1024).transpose(2, 0, 1, 3)


def solution(mesh):
    shape = (mesh.shape["lat"], mesh.shape["lon"])
    return jax.shard_map(
        functools.partial(per_device, shape),
        mesh=mesh,
        in_specs=(P(None, "lat", "lon", None), P(None, "lat", "lon")) + (P(),) * 17,
        out_specs=P(None, "lat", "lon", None),
        check_vma=False,
    )
```
